32 devices in a mesh: grp: 4 (over z), dom: 8 (over y, x, core).
Axes of the slice: x: 2, y: 2, z: 4, core: 2. Of those that a mesh axis runs over, the one named last changes fastest.
Arguments:
- parent_local: float32 [2048, 296], P(('grp', 'dom')), may hold values from -6 to 6
- parent_slot: int32 [16384], P(('grp', 'dom')), may hold values from 0 to 79, as said below
- child_octant: int32 [16384], P(('grp', 'dom')), may hold values from 0 to 7
- child_m2l: float32 [16384, 296], P(('grp', 'dom')), may hold values from -6 to 6
- l2l_ops: float32 [8, 296, 296], replicated, may hold values from -0.375 to 0.375
- leaf_center: float32 [16384, 3], P(('grp', 'dom')), may hold values from 0 to 2
- src_coords: float32 [16384, 3, 128], P(('grp', 'dom')), may hold values from 0 to 2
- src_charge: float32 [16384, 128], P(('grp', 'dom')), may hold values from -6 to 6
- obs_owner: int32 [16384], replicated, may hold values from 0 to 31, as said below
- obs_offset: float32 [32768, 3, 128], P(('grp', 'dom')), may hold values from -1 to 1
- near_slots: int32 [32768, 8], P(('grp', 'dom')), may hold values from 0 to 1023, as said below
Outputs:
- leaf_local: float32 [16384, 296], P(('grp', 'dom'))
- potential: float32 [32768, 128], P(('grp', 'dom'))
The draws below stay inside these ranges and needn't reach their ends.
Inputs may be any that keep to these rules, and one draw needn't show every extreme that they name: `parent_slot`: values below 16 name the last 16 parents of the previous device in the flat order over grp and dom; a value v of 16 or more names the device's own parent v - 16. Nondecreasing within a device; the first device names only its own parents. `obs_owner`: among one device's 512 leaves at most 32 share an owner; one owner receives exactly 32 leaves from every device. `near_slots`: the first entry of a row is the row's own index within its device; the others are rows of the same device that hold a leaf.
All inputs are finite; a program needn't handle non-finite values.
Results may differ from the reference program's by a relative error of at most 0.0003.
Values sent between devices are 32-bit elements; how exact they have to be, the bound alone decides.
No kernel may reach another device: no remote copies, remote signals or barrier semaphores. Data moves between devices by JAX's collectives and lax.ppermute only.
A program may use at most 64 MiB of HBM per device.

```python
import math
import jax
import jax.numpy as jnp
import numpy as np
from jax import lax

ORDER = 8
Q = 296
BLK = 128
NEAR = 8
RIM = 16
LEAF_DEV = 512
PAR_DEV = 64
LEAVES = 16384
PARENTS = 2048
SLOTS = 1024
OBS_ROWS = 32768
N_GRP = 4
N_DOM = 8


def owner_table(key):
    device_list = N_GRP * N_DOM
    capacity = 2 * LEAF_DEV // device_list
    slot_table = device_list * capacity
    busiest_owner = jax.random.randint(jax.random.fold_in(key, 101), (), 0, device_list)
    frequent_owners = jax.random.randint(jax.random.fold_in(key, 102), (device_list,), 0, 4) == 0
    target_owner = jnp.arange(slot_table, dtype=jnp.int32) // capacity
    extra_weight = jnp.where(frequent_owners[target_owner], 8192, 0) + jnp.where(target_owner == busiest_owner, 32768, 0)
    owner_scores = jax.random.randint(jax.random.fold_in(key, 103), (device_list, slot_table), 0, 16384) + extra_weight[None, :]
    distinct = owner_scores * slot_table + jnp.arange(slot_table, dtype=jnp.int32)[None, :]
    chosen = lax.top_k(distinct, LEAF_DEV)[1]
    owners = target_owner[chosen]
    shuffle_keys = jax.random.split(jax.random.fold_in(key, 104), device_list)
    orders = jax.vmap(lambda sub_key: jax.random.permutation(sub_key, LEAF_DEV))(shuffle_keys)
    return jnp.take_along_axis(owners, orders, axis=1).astype(jnp.int32)


def draw_obs_owner(key, part):
    return owner_table(key).reshape(-1)


def draw_near_slots(key, part):
    device_list = N_GRP * N_DOM
    capacity = 2 * LEAF_DEV // device_list
    slot_table = device_list * capacity
    owners = owner_table(key)
    counts = jnp.sum((owners[:, :, None] == jnp.arange(device_list, dtype=jnp.int32)[None, None, :]).astype(jnp.int32), axis=1)
    live_rows = (jnp.arange(capacity, dtype=jnp.int32)[None, None, :] < counts.T[:, :, None]).reshape(device_list, slot_table)
    live_count = jnp.maximum(jnp.sum(live_rows.astype(jnp.int32), axis=1), 1)
    owner_scores = jax.random.randint(jax.random.fold_in(key, 201), (device_list, slot_table), 0, 4096) + live_rows.astype(jnp.int32) * 4096
    distinct = owner_scores * slot_table + jnp.arange(slot_table, dtype=jnp.int32)[None, :]
    ordered = lax.top_k(distinct, slot_table)[1]
    picks = jax.random.randint(jax.random.fold_in(key, 202), (device_list, slot_table, NEAR - 1), 0, live_count[:, None, None])
    others = jax.vmap(lambda order_row, pick_rows: order_row[pick_rows])(ordered, picks)
    selves = jnp.broadcast_to(jnp.arange(slot_table, dtype=jnp.int32)[None, :, None], (device_list, slot_table, 1))
    return jnp.concatenate([selves, others.astype(jnp.int32)], axis=2).reshape(device_list * slot_table, NEAR)


def draw_parent_slot(key, part):
    device_list = N_GRP * N_DOM
    window = RIM + LEAF_DEV // 8
    raw_slots = jax.random.randint(jax.random.fold_in(key, 301), (device_list, LEAF_DEV), 0, window)
    lowest = jnp.where(jnp.arange(device_list, dtype=jnp.int32) == 0, RIM, 0)
    raw_slots = jnp.maximum(raw_slots, lowest[:, None])
    ordered = jnp.sort(raw_slots, axis=1)
    ordered = ordered.at[:, LEAF_DEV - 1].set(window - 1)
    ordered = ordered.at[:, 0].set(lowest)
    return ordered.reshape(-1).astype(jnp.int32)


def touch_ends(entries, own_key, least, top_value):
    dims = entries.shape
    index_at = [jax.random.randint(jax.random.fold_in(own_key, axis), (), 0, dims[axis]) for axis in range(len(dims))]
    entries = entries.at[tuple(index_at)].set(least)
    longest = dims.index(max(dims))
    index_at[longest] = (index_at[longest] + 1) % dims[longest]
    return entries.at[tuple(index_at)].set(top_value)


def levels(rng, dims, cuts, low, high):
    factor_of = 1.0
    for axis_at, shards_of in cuts:
        heights = jax.random.uniform(jax.random.fold_in(jax.random.fold_in(rng, 6), axis_at), (shards_of,), jnp.float32, low / len(cuts), high / len(cuts))
        factor_of = factor_of * jnp.repeat(jnp.exp(heights), dims[axis_at] // shards_of).reshape((-1,) + (1,) * (len(dims) - 1 - axis_at))
    return factor_of


def scatter_about(rng, dims, deviation, limit, shards=(), kind=jnp.bfloat16):
    entries = jax.random.normal(rng, dims, jnp.float32) * deviation
    if len(shards) > 0:
        entries = levels(rng, dims, shards, -0.22, 0.18) * entries
    return jnp.clip(entries, min=-limit, max=limit).astype(kind)


def setup_inputs(seed: int = 0) -> dict:
    keys = jax.random.split(jax.random.key(seed), 12)
    return {
        "parent_local": scatter_about(keys[0], (PARENTS, Q), 1.0, 6.0, ((0, 32),), jnp.float32),
        "parent_slot": draw_parent_slot(jax.random.fold_in(keys[11], 71), 0),
        "child_octant": touch_ends(jax.random.randint(keys[2], (LEAVES,), 0, 8), jax.random.fold_in(keys[2], 1), 0, 7).astype(jnp.int32),
        "child_m2l": scatter_about(keys[3], (LEAVES, Q), 1.0, 6.0, ((0, 32),), jnp.float32),
        "l2l_ops": scatter_about(keys[4], (8, Q, Q), Q ** -0.5, 0.375, (), jnp.float32),
        "leaf_center": jnp.clip(2.0 * jax.random.uniform(keys[5], (LEAVES, 3), jnp.float32) ** levels(keys[5], (LEAVES, 3), ((0, 32),), -0.2, 0.2), 0.0, 2.0),
        "src_coords": jnp.clip(2.0 * jax.random.uniform(keys[6], (LEAVES, 3, BLK), jnp.float32) ** levels(keys[6], (LEAVES, 3, BLK), ((0, 32),), -0.2, 0.2), 0.0, 2.0),
        "src_charge": scatter_about(keys[7], (LEAVES, BLK), 1.0, 6.0, ((0, 32),), jnp.float32),
        "obs_owner": draw_obs_owner(jax.random.fold_in(keys[11], 71), 0),
        "obs_offset": jnp.clip(jax.random.uniform(keys[9], (OBS_ROWS, 3, BLK), jnp.float32, -1.0, 1.0) * levels(keys[9], (OBS_ROWS, 3, BLK), ((0, 32),), -0.4, 0.0), -1.0, 1.0),
        "near_slots": draw_near_slots(jax.random.fold_in(keys[11], 71), 0),
    }


RADIUS = 2.95
half_width = 0.5
soft_sq = 0.0025
four_pi = 4.0 * math.pi

def surface_points():
    grid = np.linspace(-1.0, 1.0, ORDER)
    points = np.stack(np.meshgrid(grid, grid, grid, indexing='ij'), 0).reshape(3, -1)
    on_surface = np.max(np.abs(points), axis=0) > 1.0 - 1e-09
    return jnp.asarray(points[:, on_surface] * RADIUS, dtype=jnp.float32)

def far_block(densities, offsets):
    surface = surface_points()
    dist_sq = jnp.zeros((offsets.shape[0], surface.shape[1], offsets.shape[2]), jnp.float32)
    for component in range(3):
        separation = offsets[:, component, None, :] - surface[component][None, :, None]
        dist_sq = dist_sq + separation * separation
    kernel = 1.0 / (four_pi * half_width * jnp.sqrt(dist_sq))
    return jnp.einsum('sq,sqb->sb', densities, kernel, precision=lax.Precision.HIGHEST)

def near_block(targets, fetch_rows, neighbours):
    summed = jnp.zeros((targets.shape[0], targets.shape[2]), jnp.float32)
    for column in range(neighbours.shape[1]):
        coords, charges = fetch_rows(neighbours[:, column])
        dist_sq = jnp.full((targets.shape[0], targets.shape[2], coords.shape[2]), soft_sq, jnp.float32)
        for component in range(3):
            separation = targets[:, component, :, None] - coords[:, component, None, :]
            dist_sq = dist_sq + separation * separation
        summed = summed + lax.optimization_barrier(jnp.sum(charges[:, None, :] * lax.rsqrt(dist_sq), axis=2))
    return summed / four_pi

def reference(parent_local, parent_slot, child_octant, child_m2l, l2l_ops, leaf_center, src_coords, src_charge, obs_owner, obs_offset, near_slots):
    device_list = N_GRP * N_DOM
    capacity = SLOTS // device_list
    leaf_index = jnp.arange(LEAVES, dtype=jnp.int32)
    source_dev = leaf_index // LEAF_DEV
    parent_global = source_dev * PAR_DEV + parent_slot - RIM
    moved = jnp.einsum('pr,oqr->opq', parent_local, l2l_ops, precision=lax.Precision.HIGHEST)
    stacked = moved.reshape(8 * PARENTS, Q)
    leaf_local = child_m2l + stacked[(child_octant * PARENTS + parent_global).astype(jnp.int32)]
    owners = obs_owner.reshape(device_list, LEAF_DEV)
    onehot = (owners[:, :, None] == jnp.arange(device_list, dtype=jnp.int32)[None, None, :]).astype(jnp.int32)
    before = jnp.cumsum(onehot, axis=1) - onehot
    leaf_rank = lax.optimization_barrier(jnp.sum(before * onehot, axis=2)).reshape(LEAVES)
    slot_row = (obs_owner * SLOTS + source_dev * capacity + leaf_rank).astype(jnp.int32)
    slot_leaf = jnp.full((OBS_ROWS,), -1, jnp.int32).at[slot_row].set(leaf_index)
    receiver = jnp.arange(OBS_ROWS, dtype=jnp.int32) // SLOTS
    near_leaf = slot_leaf[(near_slots + receiver[:, None] * SLOTS).astype(jnp.int32)]

    def fetch_rows(leaves):
        is_live = leaves >= 0
        clipped = jnp.maximum(leaves, 0)
        return (src_coords[clipped], jnp.where(is_live[:, None], src_charge[clipped], 0.0))

    def one_block(pieces):
        block_leaf, offsets, block_near = pieces
        is_live = block_leaf >= 0
        clipped = jnp.maximum(block_leaf, 0)
        densities = jnp.where(is_live[:, None], leaf_local[clipped], 0.0)
        centers = leaf_center[clipped]
        targets = centers[:, :, None] + half_width * offsets
        far_part = far_block(densities, offsets)
        near_part = near_block(targets, fetch_rows, block_near)
        return jnp.where(is_live[:, None], far_part + near_part, 0.0)
    blocks = OBS_ROWS // 64
    potential = lax.map(one_block, (slot_leaf.reshape(blocks, 64), obs_offset.reshape(blocks, 64, 3, BLK), near_leaf.reshape(blocks, 64, NEAR)))
    return (leaf_local, potential.reshape(OBS_ROWS, BLK))
```

```python
import functools
import math

import jax
import jax.numpy as jnp
import numpy as np
from jax import lax
from jax.experimental import pallas as pl
from jax.experimental.pallas import tpu as pltpu
from jax.sharding import PartitionSpec as P

ORDER = 8
RIM = 16
RADIUS = 2.95
HALF_WIDTH = 0.5
SOFT_SQ = 0.0025
FOUR_PI = 4.0 * math.pi
AXES = ("grp", "dom")
FEATS = 32
GROUP = 8
UNROLL = 2
VMEM_LIMIT = 50 * 1024 * 1024

F32 = jnp.float32
BF16 = jnp.bfloat16


def from_behind(block, axis, distance):
    devices = range(lax.axis_size(axis))
    route = [(i - distance, i) for i in devices if i - distance in devices]
    return lax.ppermute(block, axis, route)


def surface_points():
    grid = np.linspace(-1.0, 1.0, ORDER)
    points = np.stack(np.meshgrid(grid, grid, grid, indexing="ij"), 0).reshape(3, -1)
    on_surface = np.max(np.abs(points), axis=0) > 1.0 - 1e-09
    return (points[:, on_surface] * RADIUS).astype(np.float32)


def surface_feats(lanes):
    points = surface_points()
    short = jnp.bfloat16

    def pieces(value):
        high = value.astype(short)
        rest = value - high.astype(np.float32)
        mid = rest.astype(short)
        low = (rest - mid.astype(np.float32)).astype(short)
        return high, mid, low

    table = np.zeros((FEATS, lanes), short)
    width = points.shape[1]
    for c in range(3):
        high, mid, low = pieces(points[c])
        for i, piece in enumerate((high, high, high, mid, mid, low)):
            table[6 * c + i, :width] = piece
    norm = np.ones((lanes,), np.float32)
    norm[:width] = np.sum(points.astype(np.float64) ** 2, axis=0).astype(np.float32)
    table[18:21] = 1.0
    for i, piece in enumerate(pieces(norm)):
        table[21 + i] = piece
    return table


def split(value):
    high = value.astype(BF16).astype(F32)
    rest = value - high
    mid = rest.astype(BF16).astype(F32)
    return high, mid, rest - mid


def put_feats(stage_ref, rows, is_target):
    for f, row in enumerate(rows):
        stage_ref[pl.ds(f, GROUP, stride=FEATS), :] = row


def point_rows(coords, extra, is_target):
    norm = coords[0] * coords[0] + coords[1] * coords[1] + coords[2] * coords[2] + extra
    ones = jnp.ones_like(norm)
    rows = []
    for value in coords:
        high, mid, low = split(-2.0 * value if is_target else value)
        rows += [high, mid, low, high, mid, high] if is_target else [high, high, high, mid, mid, low]
    norms = list(split(norm))
    rows += norms + [ones] * 3 if is_target else [ones] * 3 + norms
    return rows


def store_feats(stage_ref, out_ref, base, rows):
    for f, row in enumerate(rows):
        stage_ref[pl.ds(f, GROUP, stride=FEATS), :] = row
    out_ref[pl.ds(base, GROUP)] = stage_ref[...].reshape(GROUP, FEATS, row.shape[1]).astype(BF16)


def clear_stage(stage_ref):
    stage_ref[...] = jnp.zeros_like(stage_ref)


def lane_sums(block):
    high = block.astype(BF16)
    low = (block - high.astype(F32)).astype(BF16)
    ones = jnp.ones((8, block.shape[1]), BF16)
    dims = (((1,), (1,)), ((), ()))
    total = lax.dot_general(ones, high, dims, preferred_element_type=F32)
    total = total + lax.dot_general(ones, low, dims, preferred_element_type=F32)
    return total[0:1]


def pair_sq(left, right):
    return lax.dot_general(left, right, (((0,), (0,)), ((), ())), preferred_element_type=F32)


def pack_sources(capacity, n_dev, owner_ref, center_ref, coords_ref, charge_ref, out_ref, dest_ref, count_ref):
    rows = 4 * capacity + 8
    leaves = charge_ref.shape[0]
    lane = lax.broadcasted_iota(jnp.int32, (8, 128), 1)
    sub = lax.broadcasted_iota(jnp.int32, (8, 128), 0)

    def clear(i, carry):
        count_ref[i] = 0
        return carry

    lax.fori_loop(0, n_dev, clear, 0)

    def step(j, carry):
        owner = owner_ref[j]
        rank = count_ref[owner]
        count_ref[owner] = rank + 1
        dest_ref[j] = owner * capacity + rank
        base = owner * rows
        for c in range(3):
            out_ref[pl.ds(base + c * capacity + rank, 1), :] = coords_ref[c, pl.ds(j, 1), :]
        out_ref[pl.ds(base + 3 * capacity + rank, 1), :] = charge_ref[pl.ds(j, 1), :]
        place = pl.ds(pl.multiple_of(base + 4 * capacity, 8), 8)
        value = jnp.where(
            sub == 0,
            center_ref[j],
            jnp.where(sub == 1, center_ref[leaves + j], center_ref[2 * leaves + j]),
        )
        out_ref[place, :] = jnp.where(lane == rank, value, out_ref[place, :])
        return carry

    lax.fori_loop(0, leaves, step, 0, unroll=2)


def route_leaves(parents, index_ref, dest_ref, m2l_ref, moved_ref, leaf_ref, out_ref):
    def step(j, carry):
        row = m2l_ref[pl.ds(j, 1), :] + moved_ref[pl.ds(index_ref[j], 1), :]
        leaf_ref[pl.ds(j, 1), :] = row
        out_ref[pl.ds(dest_ref[j], 1), :] = row
        return carry

    lax.fori_loop(0, m2l_ref.shape[0], step, 0, unroll=4)


def near_kernel(capacity, n_dev, slots_ref, recv_ref, obs_ref, out_ref, source_ref, target_ref, stage_a, stage_b):
    rows = 4 * capacity + 8
    clear_stage(stage_a)
    clear_stage(stage_b)

    def prepare(s, carry):
        base = pl.multiple_of(s * rows, 8)
        centers = recv_ref[pl.ds(base + 4 * capacity, 8), :].T
        for g in range(capacity // GROUP):
            slot = pl.multiple_of(s * capacity + g * GROUP, GROUP)
            coords = [
                recv_ref[pl.ds(base + c * capacity + g * GROUP, GROUP), :] - 1.0 for c in range(3)
            ]
            store_feats(stage_a, source_ref, slot, point_rows(coords, 0.0, False))
            targets = [
                (centers[g * GROUP : (g + 1) * GROUP, c : c + 1] - 1.0)
                + HALF_WIDTH * obs_ref[c, pl.ds(slot, GROUP), :]
                for c in range(3)
            ]
            store_feats(stage_b, target_ref, slot, point_rows(targets, SOFT_SQ, True))
        return carry

    lax.fori_loop(0, n_dev, prepare, 0)

    def charge_row(slot):
        dev = slot // capacity
        return recv_ref[pl.ds(dev * rows + 3 * capacity + slot - dev * capacity, 1), :]

    def one_row(r):
        left = target_ref[r]
        total = None
        for p in range(4):
            first, second = slots_ref[8 * r + 2 * p], slots_ref[8 * r + 2 * p + 1]
            right = jnp.concatenate([source_ref[first], source_ref[second]], axis=1)
            inverse = lax.rsqrt(pair_sq(left, right))
            part = inverse[:, :128] * charge_row(first) + inverse[:, 128:] * charge_row(second)
            total = part if total is None else total + part
        out_ref[pl.ds(r, 1), :] = lane_sums(total)

    def step(i, carry):
        for u in range(UNROLL):
            one_row(i * UNROLL + u)
        return carry

    lax.fori_loop(0, out_ref.shape[0] // UNROLL, step, 0)


def far_kernel(dens_ref, obs_ref, near_ref, live_ref, surface_ref, out_ref, target_ref, stage_a):
    width = dens_ref.shape[1]
    clear_stage(stage_a)

    def prepare(g, carry):
        slot = pl.multiple_of(g * GROUP, GROUP)
        targets = [obs_ref[c, pl.ds(slot, GROUP), :] for c in range(3)]
        store_feats(stage_a, target_ref, slot, point_rows(targets, 0.0, True))
        return carry

    lax.fori_loop(0, out_ref.shape[0] // GROUP, prepare, 0)

    def one_row(r):
        inverse = lax.rsqrt(pair_sq(target_ref[r], surface_ref[...]))
        row = dens_ref[pl.ds(r, 1), :]
        total = None
        for first in range(0, width, 128):
            last = min(first + 128, width)
            part = inverse[:, first:last] * row[:, first:last]
            if last - first < 128:
                part = jnp.concatenate([part, jnp.zeros((128, 128 - last + first), F32)], axis=1)
            total = part if total is None else total + part
        return lane_sums(total)

    def step(i, carry):
        for u in range(UNROLL):
            r = i * UNROLL + u
            far = one_row(r) * (1.0 / (FOUR_PI * HALF_WIDTH))
            near = near_ref[pl.ds(r, 1), :] * (1.0 / FOUR_PI)
            out_ref[pl.ds(r, 1), :] = jnp.where(live_ref[r] > 0, far + near, 0.0)
        return carry

    lax.fori_loop(0, out_ref.shape[0] // UNROLL, step, 0)


def on_device(
    parent_local,
    parent_slot,
    child_octant,
    child_m2l,
    l2l_ops,
    leaf_center,
    src_coords,
    src_charge,
    obs_owner,
    obs_offset,
    near_slots,
):
    n_dev = lax.axis_size(AXES)
    leaf_dev, width = child_m2l.shape
    slot_table = obs_offset.shape[0]
    points = obs_offset.shape[2]
    capacity = slot_table // n_dev
    block_rows = 4 * capacity + 8
    my_index = lax.axis_index(AXES)
    vmem, smem = pl.BlockSpec(memory_space=pltpu.VMEM), pl.BlockSpec(memory_space=pltpu.SMEM)
    params = pltpu.CompilerParams(vmem_limit_bytes=VMEM_LIMIT)

    mine = lax.dynamic_slice_in_dim(obs_owner, my_index * leaf_dev, leaf_dev)
    counts = jnp.sum((obs_owner.reshape(n_dev, leaf_dev) == my_index).astype(jnp.int32), axis=1)
    live = (jnp.arange(capacity, dtype=jnp.int32)[None, :] < counts[:, None]).astype(jnp.int32).reshape(slot_table)

    packed, dest = pl.pallas_call(
        functools.partial(pack_sources, capacity, n_dev),
        out_shape=(
            jax.ShapeDtypeStruct((n_dev * block_rows, points), F32),
            jax.ShapeDtypeStruct((leaf_dev,), jnp.int32),
        ),
        in_specs=[smem, smem, vmem, vmem],
        out_specs=(vmem, smem),
        scratch_shapes=[pltpu.SMEM((n_dev,), jnp.int32)],
        compiler_params=params,
        name="pack_sources",
    )(mine, leaf_center.T.reshape(-1), src_coords.transpose(1, 0, 2), src_charge)
    recv = lax.all_to_all(
        packed.reshape(n_dev, block_rows, points), AXES, split_axis=0, concat_axis=0, tiled=True
    ).reshape(n_dev * block_rows, points)

    rim_rows = from_behind(parent_local[parent_local.shape[0] - RIM :], AXES, 1)
    parents = jnp.concatenate([rim_rows, parent_local], axis=0)
    moved = jnp.einsum("pr,oqr->opq", parents, l2l_ops, precision=lax.Precision.HIGHEST)
    stacked = moved.reshape(8 * parents.shape[0], width)
    leaf_local, packed_dens = pl.pallas_call(
        functools.partial(route_leaves, parents.shape[0]),
        out_shape=(
            jax.ShapeDtypeStruct((leaf_dev, width), F32),
            jax.ShapeDtypeStruct((slot_table, width), F32),
        ),
        in_specs=[smem, smem, vmem, vmem],
        out_specs=(vmem, vmem),
        compiler_params=params,
        name="route_leaves",
    )(child_octant * parents.shape[0] + parent_slot, dest, child_m2l, stacked)
    dens = lax.all_to_all(
        packed_dens.reshape(n_dev, capacity, width), AXES, split_axis=0, concat_axis=0, tiled=True
    ).reshape(slot_table, width)

    obs = obs_offset.transpose(1, 0, 2)
    pairs = slot_table * near_slots.shape[1] * points * points
    near = pl.pallas_call(
        functools.partial(near_kernel, capacity, n_dev),
        out_shape=jax.ShapeDtypeStruct((slot_table, points), F32),
        in_specs=[smem, vmem, vmem],
        out_specs=vmem,
        scratch_shapes=[
            pltpu.VMEM((slot_table, FEATS, points), BF16),
            pltpu.VMEM((slot_table, FEATS, points), BF16),
            pltpu.VMEM((GROUP * FEATS, points), F32),
            pltpu.VMEM((GROUP * FEATS, points), F32),
        ],
        compiler_params=params,
        cost_estimate=pl.CostEstimate(flops=70 * pairs, bytes_accessed=5 * 10**6, transcendentals=pairs),
        name="near_field",
    )(near_slots.reshape(-1), recv, obs)
    surface = jnp.asarray(surface_feats(-(-width // 128) * 128))
    potential = pl.pallas_call(
        far_kernel,
        out_shape=jax.ShapeDtypeStruct((slot_table, points), F32),
        in_specs=[vmem, vmem, vmem, smem, vmem],
        out_specs=vmem,
        scratch_shapes=[
            pltpu.VMEM((slot_table, FEATS, points), BF16),
            pltpu.VMEM((GROUP * FEATS, points), F32),
        ],
        compiler_params=params,
        cost_estimate=pl.CostEstimate(flops=10**10, bytes_accessed=5 * 10**6, transcendentals=10**7),
        name="far_field",
    )(dens, obs, near, live, surface)
    return (leaf_local, potential)


def solution(mesh):
    placed = (
        P(AXES, None),
        P(AXES),
        P(AXES),
        P(AXES, None),
        P(),
        P(AXES, None),
        P(AXES, None, None),
        P(AXES, None),
        P(),
        P(AXES, None, None),
        P(AXES, None),
    )
    return jax.shard_map(
        on_device,
        mesh=mesh,
        in_specs=placed,
        out_specs=(P(AXES, None), P(AXES, None)),
        check_vma=False,
    )
```

```python
import functools
import math

import jax
import jax.numpy as jnp
import numpy as np
from jax import lax
from jax.experimental import pallas as pl
from jax.experimental.pallas import tpu as pltpu
from jax.sharding import PartitionSpec as P

ORDER = 8
RIM = 16
RADIUS = 2.95
HALF_WIDTH = 0.5
SOFT_SQ = 0.0025
FOUR_PI = 4.0 * math.pi
AXES = ("grp", "dom")
FEATS = 32
GROUP = 8
VMEM_LIMIT = 50 * 1024 * 1024

F32 = jnp.float32
BF16 = jnp.bfloat16


def from_behind(block, axis, distance):
    devices = range(lax.axis_size(axis))
    route = [(i - distance, i) for i in devices if i - distance in devices]
    return lax.ppermute(block, axis, route)


def surface_points():
    grid = np.linspace(-1.0, 1.0, ORDER)
    points = np.stack(np.meshgrid(grid, grid, grid, indexing="ij"), 0).reshape(3, -1)
    on_surface = np.max(np.abs(points), axis=0) > 1.0 - 1e-09
    return (points[:, on_surface] * RADIUS).astype(np.float32)


def surface_feats(lanes):
    points = surface_points()
    short = jnp.bfloat16

    def pieces(value):
        high = value.astype(short)
        rest = value - high.astype(np.float32)
        mid = rest.astype(short)
        low = (rest - mid.astype(np.float32)).astype(short)
        return high, mid, low

    table = np.zeros((FEATS, lanes), short)
    width = points.shape[1]
    for c in range(3):
        high, mid, low = pieces(points[c])
        for i, piece in enumerate((high, high, high, mid, mid, low)):
            table[6 * c + i, :width] = piece
    norm = np.ones((lanes,), np.float32)
    norm[:width] = np.sum(points.astype(np.float64) ** 2, axis=0).astype(np.float32)
    table[18:21] = 1.0
    for i, piece in enumerate(pieces(norm)):
        table[21 + i] = piece
    return table


def split(value):
    high = value.astype(BF16).astype(F32)
    rest = value - high
    mid = rest.astype(BF16).astype(F32)
    return high, mid, rest - mid


def point_rows(coords, extra, is_target):
    norm = coords[0] * coords[0] + coords[1] * coords[1] + coords[2] * coords[2] + extra
    ones = jnp.ones_like(norm)
    rows = []
    for value in coords:
        high, mid, low = split(-2.0 * value if is_target else value)
        rows += [high, mid, low, high, mid, high] if is_target else [high, high, high, mid, mid, low]
    norms = list(split(norm))
    rows += norms + [ones] * 3 if is_target else [ones] * 3 + norms
    return rows


def store_feats(stage_ref, out_ref, base, rows):
    for f, row in enumerate(rows):
        stage_ref[pl.ds(f, GROUP, stride=FEATS), :] = row
    out_ref[pl.ds(base, GROUP)] = stage_ref[...].reshape(GROUP, FEATS, row.shape[1]).astype(BF16)


def clear_stage(stage_ref):
    stage_ref[...] = jnp.zeros_like(stage_ref)


def lane_sums(block):
    high = block.astype(BF16)
    low = (block - high.astype(F32)).astype(BF16)
    ones = jnp.ones((GROUP, 2 * block.shape[1]), BF16)
    pieces = jnp.concatenate([high, low], axis=1)
    return lax.dot_general(ones, pieces, (((1,), (1,)), ((), ())), preferred_element_type=F32)


def pack_sources(capacity, n_dev, owner_ref, center_ref, coords_ref, charge_ref, out_ref, dest_ref, count_ref):
    rows = 4 * capacity + 8
    leaves = charge_ref.shape[0]
    lane = lax.broadcasted_iota(jnp.int32, (8, 128), 1)
    sub = lax.broadcasted_iota(jnp.int32, (8, 128), 0)

    def clear(i, carry):
        count_ref[i] = 0
        return carry

    lax.fori_loop(0, n_dev, clear, 0)

    def step(j, carry):
        owner = owner_ref[j]
        rank = count_ref[owner]
        count_ref[owner] = rank + 1
        dest_ref[j] = owner * capacity + rank
        base = owner * rows
        for c in range(3):
            out_ref[pl.ds(base + c * capacity + rank, 1), :] = coords_ref[c, pl.ds(j, 1), :]
        out_ref[pl.ds(base + 3 * capacity + rank, 1), :] = charge_ref[pl.ds(j, 1), :]
        place = pl.ds(pl.multiple_of(base + 4 * capacity, 8), 8)
        value = jnp.where(
            sub == 0,
            center_ref[j],
            jnp.where(sub == 1, center_ref[leaves + j], center_ref[2 * leaves + j]),
        )
        out_ref[place, :] = jnp.where(lane == rank, value, out_ref[place, :])
        return carry

    lax.fori_loop(0, leaves, step, 0, unroll=2)


def route_leaves(parents, index_ref, dest_ref, m2l_ref, moved_ref, leaf_ref, out_ref):
    def step(j, carry):
        row = m2l_ref[pl.ds(j, 1), :] + moved_ref[pl.ds(index_ref[j], 1), :]
        leaf_ref[pl.ds(j, 1), :] = row
        out_ref[pl.ds(dest_ref[j], 1), :] = row
        return carry

    lax.fori_loop(0, m2l_ref.shape[0], step, 0, unroll=4)


def near_kernel(
    capacity,
    n_dev,
    slots_ref,
    recv_ref,
    obs_ref,
    out_ref,
    source_ref,
    target_ref,
    charge_ref,
    stage_a,
    stage_b,
    left_a,
    left_b,
    total_a,
    total_b,
):
    rows = 4 * capacity + 8
    blocks = out_ref.shape[0] // GROUP
    sub = lax.broadcasted_iota(jnp.int32, (GROUP, out_ref.shape[1]), 0)
    clear_stage(stage_a)
    clear_stage(stage_b)

    def prepare(s, carry):
        base = pl.multiple_of(s * rows, 8)
        centers = recv_ref[pl.ds(base + 4 * capacity, 8), :].T
        for g in range(capacity // GROUP):
            slot = pl.multiple_of(s * capacity + g * GROUP, GROUP)
            coords = [
                recv_ref[pl.ds(base + c * capacity + g * GROUP, GROUP), :] - 1.0 for c in range(3)
            ]
            store_feats(stage_a, source_ref, slot, point_rows(coords, 0.0, False))
            targets = [
                (centers[g * GROUP : (g + 1) * GROUP, c : c + 1] - 1.0)
                + HALF_WIDTH * obs_ref[c, pl.ds(slot, GROUP), :]
                for c in range(3)
            ]
            store_feats(stage_b, target_ref, slot, point_rows(targets, SOFT_SQ, True))
            charge_ref[pl.ds(slot, GROUP), :] = recv_ref[
                pl.ds(base + 3 * capacity + g * GROUP, GROUP), :
            ]
        return carry

    lax.fori_loop(0, n_dev, prepare, 0)

    def turn(block, u, left_ref):
        left_ref[u] = target_ref[block * GROUP + u].T

    def pair_work(block, u, left_ref, total_ref):
        left = left_ref[u]
        at = (block * GROUP + u) * GROUP
        total = None
        for p in range(4):
            first, second = slots_ref[at + 2 * p], slots_ref[at + 2 * p + 1]
            right = jnp.concatenate([source_ref[first], source_ref[second]], axis=1)
            inverse = lax.rsqrt(jnp.dot(left, right, preferred_element_type=F32))
            part = (
                inverse[:, :128] * charge_ref[pl.ds(first, 1), :]
                + inverse[:, 128:] * charge_ref[pl.ds(second, 1), :]
            )
            total = part if total is None else total + part
        total_ref[u] = total

    def half(before, block, after, left_now, left_next, total_before, total_now):
        sums = None
        for u in range(GROUP):
            turn(after, u, left_next)
            pair_work(block, u, left_now, total_now)
            part = lane_sums(total_before[u])
            sums = part if sums is None else jnp.where(sub == u, part, sums)
        out_ref[pl.ds(pl.multiple_of(before * GROUP, GROUP), GROUP), :] = sums

    for u in range(GROUP):
        turn(0, u, left_a)
    total_b[...] = jnp.zeros_like(total_b)

    def step(i, carry):
        one, two = 2 * i, 2 * i + 1
        half(jnp.maximum(one - 1, 0), one, two, left_a, left_b, total_b, total_a)
        half(one, two, jnp.minimum(two + 1, blocks - 1), left_b, left_a, total_a, total_b)
        return carry

    lax.fori_loop(0, blocks // 2, step, 0)
    sums = None
    for u in range(GROUP):
        part = lane_sums(total_b[u])
        sums = part if sums is None else jnp.where(sub == u, part, sums)
    out_ref[pl.ds((blocks - 1) * GROUP, GROUP), :] = sums


def far_kernel(dens_ref, obs_ref, near_ref, live_ref, surface_ref, out_ref, target_ref, turned_ref, stage_a):
    width = dens_ref.shape[1]
    points = out_ref.shape[1]
    clear_stage(stage_a)

    def prepare(g, carry):
        slot = pl.multiple_of(g * GROUP, GROUP)
        targets = [obs_ref[c, pl.ds(slot, GROUP), :] for c in range(3)]
        store_feats(stage_a, target_ref, slot, point_rows(targets, 0.0, True))
        return carry

    lax.fori_loop(0, out_ref.shape[0] // GROUP, prepare, 0)
    sub = lax.broadcasted_iota(jnp.int32, (GROUP, points), 0)

    def tile(t, carry):
        first_row = pl.multiple_of(t * 128, 128)
        turned_ref[...] = dens_ref[pl.ds(first_row, 128), :].T

        def group(g, carry):
            dens = pltpu.roll(turned_ref[...], lax.rem(128 - g * GROUP, 128), 1)
            slot = pl.multiple_of(first_row + g * GROUP, GROUP)
            far = jnp.zeros((GROUP, points), F32)
            for u in range(0, GROUP, 2):
                right = jnp.concatenate([target_ref[slot + u], target_ref[slot + u + 1]], axis=1)
                inverse = lax.rsqrt(jnp.dot(surface_ref[...], right, preferred_element_type=F32))
                for v in range(2):
                    terms = inverse[:, v * points : (v + 1) * points] * dens[:, u + v : u + v + 1]
                    row = jnp.sum(terms, axis=0, keepdims=True)
                    far = jnp.where(sub == u + v, row, far)
            near = near_ref[pl.ds(slot, GROUP), :]
            total = far * (1.0 / (FOUR_PI * HALF_WIDTH)) + near * (1.0 / FOUR_PI)
            alive = jnp.zeros((GROUP, points), jnp.int32)
            for u in range(GROUP):
                alive = jnp.where(sub == u, live_ref[slot + u], alive)
            out_ref[pl.ds(slot, GROUP), :] = jnp.where(alive > 0, total, 0.0)
            return carry

        lax.fori_loop(0, 128 // GROUP, group, 0)
        return carry

    lax.fori_loop(0, out_ref.shape[0] // 128, tile, 0)


def on_device(
    parent_local,
    parent_slot,
    child_octant,
    child_m2l,
    l2l_ops,
    leaf_center,
    src_coords,
    src_charge,
    obs_owner,
    obs_offset,
    near_slots,
):
    n_dev = lax.axis_size(AXES)
    leaf_dev, width = child_m2l.shape
    slot_table = obs_offset.shape[0]
    points = obs_offset.shape[2]
    capacity = slot_table // n_dev
    block_rows = 4 * capacity + 8
    my_index = lax.axis_index(AXES)
    vmem, smem = pl.BlockSpec(memory_space=pltpu.VMEM), pl.BlockSpec(memory_space=pltpu.SMEM)
    params = pltpu.CompilerParams(vmem_limit_bytes=VMEM_LIMIT)

    mine = lax.dynamic_slice_in_dim(obs_owner, my_index * leaf_dev, leaf_dev)
    counts = jnp.sum((obs_owner.reshape(n_dev, leaf_dev) == my_index).astype(jnp.int32), axis=1)
    live = (jnp.arange(capacity, dtype=jnp.int32)[None, :] < counts[:, None]).astype(jnp.int32).reshape(slot_table)

    packed, dest = pl.pallas_call(
        functools.partial(pack_sources, capacity, n_dev),
        out_shape=(
            jax.ShapeDtypeStruct((n_dev * block_rows, points), F32),
            jax.ShapeDtypeStruct((leaf_dev,), jnp.int32),
        ),
        in_specs=[smem, smem, vmem, vmem],
        out_specs=(vmem, smem),
        scratch_shapes=[pltpu.SMEM((n_dev,), jnp.int32)],
        compiler_params=params,
        name="pack_sources",
    )(mine, leaf_center.T.reshape(-1), src_coords.transpose(1, 0, 2), src_charge)
    recv = lax.all_to_all(
        packed.reshape(n_dev, block_rows, points), AXES, split_axis=0, concat_axis=0, tiled=True
    ).reshape(n_dev * block_rows, points)

    rim_rows = from_behind(parent_local[parent_local.shape[0] - RIM :], AXES, 1)
    parents = jnp.concatenate([rim_rows, parent_local], axis=0)
    moved = jnp.einsum("pr,oqr->opq", parents, l2l_ops, precision=lax.Precision.HIGHEST)
    stacked = moved.reshape(8 * parents.shape[0], width)
    leaf_local, packed_dens = pl.pallas_call(
        functools.partial(route_leaves, parents.shape[0]),
        out_shape=(
            jax.ShapeDtypeStruct((leaf_dev, width), F32),
            jax.ShapeDtypeStruct((slot_table, width), F32),
        ),
        in_specs=[smem, smem, vmem, vmem],
        out_specs=(vmem, vmem),
        compiler_params=params,
        name="route_leaves",
    )(child_octant * parents.shape[0] + parent_slot, dest, child_m2l, stacked)
    dens = lax.all_to_all(
        packed_dens.reshape(n_dev, capacity, width), AXES, split_axis=0, concat_axis=0, tiled=True
    ).reshape(slot_table, width)

    obs = obs_offset.transpose(1, 0, 2)
    pairs = slot_table * near_slots.shape[1] * points * points
    near = pl.pallas_call(
        functools.partial(near_kernel, capacity, n_dev),
        out_shape=jax.ShapeDtypeStruct((slot_table, points), F32),
        in_specs=[smem, vmem, vmem],
        out_specs=vmem,
        scratch_shapes=[
            pltpu.VMEM((slot_table, FEATS, points), BF16),
            pltpu.VMEM((slot_table, FEATS, points), BF16),
            pltpu.VMEM((slot_table, points), F32),
            pltpu.VMEM((GROUP * FEATS, points), F32),
            pltpu.VMEM((GROUP * FEATS, points), F32),
            pltpu.VMEM((GROUP, points, FEATS), BF16),
            pltpu.VMEM((GROUP, points, FEATS), BF16),
            pltpu.VMEM((GROUP, points, points), F32),
            pltpu.VMEM((GROUP, points, points), F32),
        ],
        compiler_params=params,
        cost_estimate=pl.CostEstimate(flops=70 * pairs, bytes_accessed=5 * 10**6, transcendentals=pairs),
        name="near_field",
    )(near_slots.reshape(-1), recv, obs)
    surface = jnp.asarray(surface_feats(width).T)
    potential = pl.pallas_call(
        far_kernel,
        out_shape=jax.ShapeDtypeStruct((slot_table, points), F32),
        in_specs=[vmem, vmem, vmem, smem, vmem],
        out_specs=vmem,
        scratch_shapes=[
            pltpu.VMEM((slot_table, FEATS, points), BF16),
            pltpu.VMEM((width, 128), F32),
            pltpu.VMEM((GROUP * FEATS, points), F32),
        ],
        compiler_params=params,
        cost_estimate=pl.CostEstimate(flops=10**10, bytes_accessed=5 * 10**6, transcendentals=10**7),
        name="far_field",
    )(dens, obs, near, live, surface)
    return (leaf_local, potential)


def solution(mesh):
    placed = (
        P(AXES, None),
        P(AXES),
        P(AXES),
        P(AXES, None),
        P(),
        P(AXES, None),
        P(AXES, None, None),
        P(AXES, None),
        P(),
        P(AXES, None, None),
        P(AXES, None),
    )
    return jax.shard_map(
        on_device,
        mesh=mesh,
        in_specs=placed,
        out_specs=(P(AXES, None), P(AXES, None)),
        check_vma=False,
    )
```

```python
import functools
import math

import jax
import jax.numpy as jnp
import numpy as np
from jax import lax
from jax.experimental import pallas as pl
from jax.experimental.pallas import tpu as pltpu
from jax.sharding import PartitionSpec as P

ORDER = 8
RIM = 16
RADIUS = 2.95
HALF_WIDTH = 0.5
SOFT_SQ = 0.0025
FOUR_PI = 4.0 * math.pi
AXES = ("grp", "dom")
FEATS = 32
GROUP = 8
VMEM_LIMIT = 50 * 1024 * 1024

F32 = jnp.float32
BF16 = jnp.bfloat16


def from_behind(block, axis, distance):
    devices = range(lax.axis_size(axis))
    route = [(i - distance, i) for i in devices if i - distance in devices]
    return lax.ppermute(block, axis, route)


def surface_grid():
    axis = (np.linspace(-1.0, 1.0, ORDER) * RADIUS).astype(np.float32)
    ends = (0, ORDER - 1)
    points = [
        (i, j, k)
        for i in range(ORDER)
        for j in range(ORDER)
        for k in range(ORDER)
        if i in ends or j in ends or k in ends
    ]
    return [float(value) for value in axis], points


def split(value):
    high = value.astype(BF16).astype(F32)
    rest = value - high
    mid = rest.astype(BF16).astype(F32)
    return high, mid, rest - mid


def point_rows(coords, extra, is_target):
    norm = coords[0] * coords[0] + coords[1] * coords[1] + coords[2] * coords[2] + extra
    ones = jnp.ones_like(norm)
    rows = []
    for value in coords:
        high, mid, low = split(-2.0 * value if is_target else value)
        rows += [high, mid, low, high, mid, high] if is_target else [high, high, high, mid, mid, low]
    norms = list(split(norm))
    rows += norms + [ones] * 3 if is_target else [ones] * 3 + norms
    return rows


def store_feats(stage_ref, out_ref, base, rows):
    for f, row in enumerate(rows):
        stage_ref[pl.ds(f, GROUP, stride=FEATS), :] = row
    out_ref[pl.ds(base, GROUP)] = stage_ref[...].reshape(GROUP, FEATS, row.shape[1]).astype(BF16)


def clear_stage(stage_ref):
    stage_ref[...] = jnp.zeros_like(stage_ref)


def lane_sums(block):
    high = block.astype(BF16)
    low = (block - high.astype(F32)).astype(BF16)
    ones = jnp.ones((GROUP, 2 * block.shape[1]), BF16)
    pieces = jnp.concatenate([high, low], axis=1)
    return lax.dot_general(ones, pieces, (((1,), (1,)), ((), ())), preferred_element_type=F32)


def pack_sources(capacity, owner_ref, rank_ref, center_ref, coords_ref, charge_ref, out_ref):
    rows = 4 * capacity + 8
    leaves = charge_ref.shape[0]
    lane = lax.broadcasted_iota(jnp.int32, (8, 128), 1)
    sub = lax.broadcasted_iota(jnp.int32, (8, 128), 0)

    def step(j, carry):
        rank = rank_ref[j]
        base = owner_ref[j] * rows
        for c in range(3):
            out_ref[pl.ds(base + c * capacity + rank, 1), :] = coords_ref[c, pl.ds(j, 1), :]
        out_ref[pl.ds(base + 3 * capacity + rank, 1), :] = charge_ref[pl.ds(j, 1), :]
        place = pl.ds(pl.multiple_of(base + 4 * capacity, 8), 8)
        value = jnp.where(
            sub == 0,
            center_ref[j],
            jnp.where(sub == 1, center_ref[leaves + j], center_ref[2 * leaves + j]),
        )
        out_ref[place, :] = jnp.where(lane == rank, value, out_ref[place, :])
        return carry

    lax.fori_loop(0, leaves, step, 0, unroll=4)


def route_leaves(index_ref, dest_ref, m2l_ref, moved_ref, leaf_ref, out_ref):
    def step(j, carry):
        row = m2l_ref[pl.ds(j, 1), :] + moved_ref[pl.ds(index_ref[j], 1), :]
        leaf_ref[pl.ds(j, 1), :] = row
        out_ref[pl.ds(dest_ref[j], 1), : row.shape[1]] = row
        return carry

    lax.fori_loop(0, m2l_ref.shape[0], step, 0, unroll=4)


def near_kernel(
    capacity,
    n_dev,
    slots_ref,
    recv_ref,
    obs_ref,
    out_ref,
    source_ref,
    target_ref,
    charge_ref,
    stage_a,
    stage_b,
    left_a,
    left_b,
    total_a,
    total_b,
):
    rows = 4 * capacity + 8
    blocks = out_ref.shape[0] // GROUP
    sub = lax.broadcasted_iota(jnp.int32, (GROUP, out_ref.shape[1]), 0)
    clear_stage(stage_a)
    clear_stage(stage_b)

    def prepare(s, carry):
        base = pl.multiple_of(s * rows, 8)
        centers = recv_ref[pl.ds(base + 4 * capacity, 8), :].T
        for g in range(capacity // GROUP):
            slot = pl.multiple_of(s * capacity + g * GROUP, GROUP)
            coords = [
                recv_ref[pl.ds(base + c * capacity + g * GROUP, GROUP), :] - 1.0 for c in range(3)
            ]
            store_feats(stage_a, source_ref, slot, point_rows(coords, 0.0, False))
            targets = [
                (centers[g * GROUP : (g + 1) * GROUP, c : c + 1] - 1.0)
                + HALF_WIDTH * obs_ref[c, pl.ds(slot, GROUP), :]
                for c in range(3)
            ]
            store_feats(stage_b, target_ref, slot, point_rows(targets, SOFT_SQ, True))
            charge_ref[pl.ds(slot, GROUP), :] = recv_ref[
                pl.ds(base + 3 * capacity + g * GROUP, GROUP), :
            ]
        return carry

    lax.fori_loop(0, n_dev, prepare, 0)

    def turn(block, u, left_ref):
        left_ref[u] = target_ref[block * GROUP + u].T

    def pair_work(block, u, left_ref, total_ref):
        left = left_ref[u]
        at = (block * GROUP + u) * GROUP
        total = None
        for p in range(4):
            first, second = slots_ref[at + 2 * p], slots_ref[at + 2 * p + 1]
            right = jnp.concatenate([source_ref[first], source_ref[second]], axis=1)
            inverse = lax.rsqrt(jnp.dot(left, right, preferred_element_type=F32))
            part = (
                inverse[:, :128] * charge_ref[pl.ds(first, 1), :]
                + inverse[:, 128:] * charge_ref[pl.ds(second, 1), :]
            )
            total = part if total is None else total + part
        total_ref[u] = total

    def half(before, block, after, left_now, left_next, total_before, total_now):
        sums = None
        for u in range(GROUP):
            turn(after, u, left_next)
            pair_work(block, u, left_now, total_now)
            part = lane_sums(total_before[u])
            sums = part if sums is None else jnp.where(sub == u, part, sums)
        out_ref[pl.ds(pl.multiple_of(before * GROUP, GROUP), GROUP), :] = sums

    for u in range(GROUP):
        turn(0, u, left_a)
    total_b[...] = jnp.zeros_like(total_b)

    def step(i, carry):
        one, two = 2 * i, 2 * i + 1
        half(jnp.maximum(one - 1, 0), one, two, left_a, left_b, total_b, total_a)
        half(one, two, jnp.minimum(two + 1, blocks - 1), left_b, left_a, total_a, total_b)
        return carry

    lax.fori_loop(0, blocks // 2, step, 0)
    sums = None
    for u in range(GROUP):
        part = lane_sums(total_b[u])
        sums = part if sums is None else jnp.where(sub == u, part, sums)
    out_ref[pl.ds((blocks - 1) * GROUP, GROUP), :] = sums


def far_kernel(dens_ref, obs_ref, near_ref, live_ref, out_ref, turned_ref, point_ref, far_ref):
    axis, surface = surface_grid()
    number = {point: q for q, point in enumerate(surface)}
    side = out_ref.shape[1]

    def tile(t, carry):
        first = pl.multiple_of(t * side, side)
        for column in range(0, dens_ref.shape[1], side):
            turned_ref[pl.ds(column, side), :] = dens_ref[pl.ds(first, side), pl.ds(column, side)].T
        for c in range(3):
            point_ref[c] = obs_ref[c, pl.ds(first, side), :].T

        def points(b, carry):
            place = pl.ds(pl.multiple_of(b * GROUP, GROUP), GROUP)
            squares = []
            for c in range(3):
                value = point_ref[c, place, :]
                squares.append([(value - at) * (value - at) for at in axis])
            totals = [jnp.zeros((GROUP, side), F32) for _ in range(4)]
            turn = 0
            for j in range(ORDER):
                for k in range(ORDER):
                    partial = squares[1][j] + squares[2][k]
                    for i in range(ORDER):
                        q = number.get((i, j, k))
                        if q is None:
                            continue
                        inverse = lax.rsqrt(squares[0][i] + partial)
                        totals[turn] = totals[turn] + inverse * turned_ref[pl.ds(q, 1), :]
                        turn = (turn + 1) % 4
            far_ref[place, :] = (totals[0] + totals[1]) + (totals[2] + totals[3])
            return carry

        lax.fori_loop(0, side // GROUP, points, 0)
        near = near_ref[pl.ds(first, side), :].T
        total = far_ref[...] * (1.0 / (FOUR_PI * HALF_WIDTH)) + near * (1.0 / FOUR_PI)
        total = jnp.where(live_ref[pl.ds(t, 1), :] > 0, total, 0.0)
        out_ref[pl.ds(first, side), :] = total.T
        return carry

    lax.fori_loop(0, out_ref.shape[0] // side, tile, 0)


def on_device(
    parent_local,
    parent_slot,
    child_octant,
    child_m2l,
    l2l_ops,
    leaf_center,
    src_coords,
    src_charge,
    obs_owner,
    obs_offset,
    near_slots,
):
    n_dev = lax.axis_size(AXES)
    leaf_dev, width = child_m2l.shape
    slot_table = obs_offset.shape[0]
    points = obs_offset.shape[2]
    capacity = slot_table // n_dev
    block_rows = 4 * capacity + 8
    lanes = -(-width // points) * points
    my_index = lax.axis_index(AXES)
    vmem, smem = pl.BlockSpec(memory_space=pltpu.VMEM), pl.BlockSpec(memory_space=pltpu.SMEM)
    params = pltpu.CompilerParams(vmem_limit_bytes=VMEM_LIMIT)

    mine = lax.dynamic_slice_in_dim(obs_owner, my_index * leaf_dev, leaf_dev)
    counts = jnp.sum((obs_owner.reshape(n_dev, leaf_dev) == my_index).astype(jnp.int32), axis=1)
    live = (jnp.arange(capacity, dtype=jnp.int32)[None, :] < counts[:, None]).astype(jnp.int32).reshape(slot_table)

    leaf_at = jnp.arange(leaf_dev, dtype=jnp.int32)
    same = (mine[:, None] == mine[None, :]) & (leaf_at[None, :] < leaf_at[:, None])
    rank = jnp.sum(same.astype(jnp.int32), axis=1)
    packed = pl.pallas_call(
        functools.partial(pack_sources, capacity),
        out_shape=jax.ShapeDtypeStruct((n_dev * block_rows, points), F32),
        in_specs=[smem, smem, smem, vmem, vmem],
        out_specs=vmem,
        compiler_params=params,
        name="pack_sources",
    )(mine, rank, leaf_center.T.reshape(-1), src_coords.transpose(1, 0, 2), src_charge)
    recv = lax.all_to_all(
        packed.reshape(n_dev, block_rows, points), AXES, split_axis=0, concat_axis=0, tiled=True
    ).reshape(n_dev * block_rows, points)

    rim_rows = from_behind(parent_local[parent_local.shape[0] - RIM :], AXES, 1)
    parents = jnp.concatenate([rim_rows, parent_local], axis=0)
    moved = jnp.einsum("pr,oqr->opq", parents, l2l_ops, precision=lax.Precision.HIGHEST)
    stacked = moved.reshape(8 * parents.shape[0], width)
    leaf_local, packed_dens = pl.pallas_call(
        route_leaves,
        out_shape=(
            jax.ShapeDtypeStruct((leaf_dev, width), F32),
            jax.ShapeDtypeStruct((slot_table, lanes), F32),
        ),
        in_specs=[smem, smem, vmem, vmem],
        out_specs=(vmem, vmem),
        compiler_params=params,
        name="route_leaves",
    )(child_octant * parents.shape[0] + parent_slot, mine * capacity + rank, child_m2l, stacked)
    dens = lax.all_to_all(
        packed_dens.reshape(n_dev, capacity, lanes), AXES, split_axis=0, concat_axis=0, tiled=True
    ).reshape(slot_table, lanes)

    obs = obs_offset.transpose(1, 0, 2)
    pairs = slot_table * near_slots.shape[1] * points * points
    near = pl.pallas_call(
        functools.partial(near_kernel, capacity, n_dev),
        out_shape=jax.ShapeDtypeStruct((slot_table, points), F32),
        in_specs=[smem, vmem, vmem],
        out_specs=vmem,
        scratch_shapes=[
            pltpu.VMEM((slot_table, FEATS, points), BF16),
            pltpu.VMEM((slot_table, FEATS, points), BF16),
            pltpu.VMEM((slot_table, points), F32),
            pltpu.VMEM((GROUP * FEATS, points), F32),
            pltpu.VMEM((GROUP * FEATS, points), F32),
            pltpu.VMEM((GROUP, points, FEATS), BF16),
            pltpu.VMEM((GROUP, points, FEATS), BF16),
            pltpu.VMEM((GROUP, points, points), F32),
            pltpu.VMEM((GROUP, points, points), F32),
        ],
        compiler_params=params,
        cost_estimate=pl.CostEstimate(flops=70 * pairs, bytes_accessed=5 * 10**6, transcendentals=pairs),
        name="near_field",
    )(near_slots.reshape(-1), recv, obs)
    potential = pl.pallas_call(
        far_kernel,
        out_shape=jax.ShapeDtypeStruct((slot_table, points), F32),
        in_specs=[vmem, vmem, vmem, vmem],
        out_specs=vmem,
        scratch_shapes=[
            pltpu.VMEM((lanes, points), F32),
            pltpu.VMEM((3, points, points), F32),
            pltpu.VMEM((points, points), F32),
        ],
        compiler_params=params,
        cost_estimate=pl.CostEstimate(flops=10**10, bytes_accessed=5 * 10**6, transcendentals=10**7),
        name="far_field",
    )(dens, obs, near, live.reshape(slot_table // points, points))
    return (leaf_local, potential)


def solution(mesh):
    placed = (
        P(AXES, None),
        P(AXES),
        P(AXES),
        P(AXES, None),
        P(),
        P(AXES, None),
        P(AXES, None, None),
        P(AXES, None),
        P(),
        P(AXES, None, None),
        P(AXES, None),
    )
    return jax.shard_map(
        on_device,
        mesh=mesh,
        in_specs=placed,
        out_specs=(P(AXES, None), P(AXES, None)),
        check_vma=False,
    )
```

```python
import functools
import math

import jax
import jax.numpy as jnp
import numpy as np
from jax import lax
from jax.experimental import pallas as pl
from jax.experimental.pallas import tpu as pltpu
from jax.sharding import PartitionSpec as P

ORDER = 8
RIM = 16
RADIUS = 2.95
HALF_WIDTH = 0.5
SOFT_SQ = 0.0025
FOUR_PI = 4.0 * math.pi
AXES = ("grp", "dom")
FEATS = 32
GROUP = 8
VMEM_LIMIT = 50 * 1024 * 1024

F32 = jnp.float32
BF16 = jnp.bfloat16


def from_behind(block, axis, distance):
    devices = range(lax.axis_size(axis))
    route = [(i - distance, i) for i in devices if i - distance in devices]
    return lax.ppermute(block, axis, route)


def surface_grid():
    axis = (np.linspace(-1.0, 1.0, ORDER) * RADIUS).astype(np.float32)
    ends = (0, ORDER - 1)
    points = [
        (i, j, k)
        for i in range(ORDER)
        for j in range(ORDER)
        for k in range(ORDER)
        if i in ends or j in ends or k in ends
    ]
    return [float(value) for value in axis], points


def split(value):
    high = value.astype(BF16).astype(F32)
    rest = value - high
    mid = rest.astype(BF16).astype(F32)
    return high, mid, rest - mid


def point_rows(coords, extra, is_target):
    norm = coords[0] * coords[0] + coords[1] * coords[1] + coords[2] * coords[2] + extra
    ones = jnp.ones_like(norm)
    rows = []
    for value in coords:
        high, mid, low = split(-2.0 * value if is_target else value)
        rows += [high, mid, low, high, mid, high] if is_target else [high, high, high, mid, mid, low]
    norms = list(split(norm))
    rows += norms + [ones] * 3 if is_target else [ones] * 3 + norms
    return rows


def store_feats(stage_ref, out_ref, base, rows):
    for f, row in enumerate(rows):
        stage_ref[pl.ds(f, GROUP, stride=FEATS), :] = row
    out_ref[pl.ds(base, GROUP)] = stage_ref[...].reshape(GROUP, FEATS, row.shape[1]).astype(BF16)


def clear_stage(stage_ref):
    stage_ref[...] = jnp.zeros_like(stage_ref)


def pack_sources(capacity, owner_ref, rank_ref, center_ref, coords_ref, charge_ref, out_ref):
    rows = 4 * capacity + 8
    leaves = charge_ref.shape[0]
    lane = lax.broadcasted_iota(jnp.int32, (8, 128), 1)
    sub = lax.broadcasted_iota(jnp.int32, (8, 128), 0)

    def step(j, carry):
        rank = rank_ref[j]
        base = owner_ref[j] * rows
        for c in range(3):
            out_ref[pl.ds(base + c * capacity + rank, 1), :] = coords_ref[c, pl.ds(j, 1), :]
        out_ref[pl.ds(base + 3 * capacity + rank, 1), :] = charge_ref[pl.ds(j, 1), :]
        place = pl.ds(pl.multiple_of(base + 4 * capacity, 8), 8)
        value = jnp.where(
            sub == 0,
            center_ref[j],
            jnp.where(sub == 1, center_ref[leaves + j], center_ref[2 * leaves + j]),
        )
        out_ref[place, :] = jnp.where(lane == rank, value, out_ref[place, :])
        return carry

    lax.fori_loop(0, leaves, step, 0, unroll=4)


def route_leaves(index_ref, dest_ref, m2l_ref, moved_ref, leaf_ref, out_ref):
    def step(j, carry):
        row = m2l_ref[pl.ds(j, 1), :] + moved_ref[pl.ds(index_ref[j], 1), :]
        leaf_ref[pl.ds(j, 1), :] = row
        out_ref[pl.ds(dest_ref[j], 1), : row.shape[1]] = row
        return carry

    lax.fori_loop(0, m2l_ref.shape[0], step, 0, unroll=4)


def near_kernel(
    capacity,
    n_dev,
    slots_ref,
    recv_ref,
    obs_ref,
    out_ref,
    source_ref,
    target_ref,
    charge_ref,
    stage_a,
    stage_b,
    left_a,
    left_b,
    total_a,
    total_b,
):
    rows = 4 * capacity + 8
    blocks = out_ref.shape[0] // GROUP
    side = out_ref.shape[1]
    lane = lax.broadcasted_iota(jnp.int32, (side, side), 1)
    clear_stage(stage_a)
    clear_stage(stage_b)

    def prepare(s, carry):
        base = pl.multiple_of(s * rows, 8)
        centers = recv_ref[pl.ds(base + 4 * capacity, 8), :].T
        for g in range(capacity // GROUP):
            slot = pl.multiple_of(s * capacity + g * GROUP, GROUP)
            coords = [
                recv_ref[pl.ds(base + c * capacity + g * GROUP, GROUP), :] - 1.0 for c in range(3)
            ]
            store_feats(stage_a, source_ref, slot, point_rows(coords, 0.0, False))
            targets = [
                (centers[g * GROUP : (g + 1) * GROUP, c : c + 1] - 1.0)
                + HALF_WIDTH * obs_ref[c, pl.ds(slot, GROUP), :]
                for c in range(3)
            ]
            store_feats(stage_b, target_ref, slot, point_rows(targets, SOFT_SQ, True))
            charge_ref[pl.ds(slot, GROUP), :] = recv_ref[
                pl.ds(base + 3 * capacity + g * GROUP, GROUP), :
            ]
        return carry

    lax.fori_loop(0, n_dev, prepare, 0)

    def turn(block, u, left_ref):
        left_ref[u] = target_ref[block * GROUP + u].T

    def pair_work(block, u, left_ref, total_ref):
        left = left_ref[u]
        at = (block * GROUP + u) * GROUP
        total = None
        for p in range(4):
            first, second = slots_ref[at + 2 * p], slots_ref[at + 2 * p + 1]
            right = jnp.concatenate([source_ref[first], source_ref[second]], axis=1)
            inverse = lax.rsqrt(jnp.dot(left, right, preferred_element_type=F32))
            part = (
                inverse[:, :128] * charge_ref[pl.ds(first, 1), :]
                + inverse[:, 128:] * charge_ref[pl.ds(second, 1), :]
            )
            total = part if total is None else total + part
        total_ref[u] = total

    def put_sums(block, total_ref):
        tile, column = block * GROUP // side, lax.rem(block * GROUP, side)
        place = pl.ds(pl.multiple_of(tile * side, side), side)

        def add_row(sums, u):
            row = jnp.sum(total_ref[u], axis=1, keepdims=True)
            return jnp.where(lane == column + u, row, sums)

        def finish(sums):
            out_ref[place, :] = sums

        return out_ref[place, :], add_row, finish

    def half(before, block, after, left_now, left_next, total_before, total_now):
        sums, add_row, finish = put_sums(before, total_before)
        for u in range(GROUP):
            turn(after, u, left_next)
            pair_work(block, u, left_now, total_now)
            sums = add_row(sums, u)
        finish(sums)

    for u in range(GROUP):
        turn(0, u, left_a)
    total_b[...] = jnp.zeros_like(total_b)

    def step(i, carry):
        one, two = 2 * i, 2 * i + 1
        half(jnp.maximum(one - 1, 0), one, two, left_a, left_b, total_b, total_a)
        half(one, two, jnp.minimum(two + 1, blocks - 1), left_b, left_a, total_a, total_b)
        return carry

    lax.fori_loop(0, blocks // 2, step, 0)
    sums, add_row, finish = put_sums(blocks - 1, total_b)
    for u in range(GROUP):
        sums = add_row(sums, u)
    finish(sums)


def far_kernel(dens_ref, obs_ref, near_ref, live_ref, out_ref, turned_ref, point_ref, far_ref):
    axis, surface = surface_grid()
    number = {point: q for q, point in enumerate(surface)}
    side = out_ref.shape[1]

    def tile(t, carry):
        first = pl.multiple_of(t * side, side)
        for column in range(0, dens_ref.shape[1], side):
            turned_ref[pl.ds(column, side), :] = dens_ref[pl.ds(first, side), pl.ds(column, side)].T
        for c in range(3):
            point_ref[c] = obs_ref[c, pl.ds(first, side), :].T

        def points(b, carry):
            place = pl.ds(pl.multiple_of(b * GROUP, GROUP), GROUP)
            squares = []
            for c in range(3):
                value = point_ref[c, place, :]
                squares.append([(value - at) * (value - at) for at in axis])
            totals = [jnp.zeros((GROUP, side), F32) for _ in range(4)]
            turn = 0
            for j in range(ORDER):
                for k in range(ORDER):
                    partial = squares[1][j] + squares[2][k]
                    for i in range(ORDER):
                        q = number.get((i, j, k))
                        if q is None:
                            continue
                        inverse = lax.rsqrt(squares[0][i] + partial)
                        totals[turn] = totals[turn] + inverse * turned_ref[pl.ds(q, 1), :]
                        turn = (turn + 1) % 4
            far_ref[place, :] = (totals[0] + totals[1]) + (totals[2] + totals[3])
            return carry

        lax.fori_loop(0, side // GROUP, points, 0)
        near = near_ref[pl.ds(first, side), :]
        total = far_ref[...] * (1.0 / (FOUR_PI * HALF_WIDTH)) + near * (1.0 / FOUR_PI)
        total = jnp.where(live_ref[pl.ds(t, 1), :] > 0, total, 0.0)
        out_ref[pl.ds(first, side), :] = total.T
        return carry

    lax.fori_loop(0, out_ref.shape[0] // side, tile, 0)


def on_device(
    parent_local,
    parent_slot,
    child_octant,
    child_m2l,
    l2l_ops,
    leaf_center,
    src_coords,
    src_charge,
    obs_owner,
    obs_offset,
    near_slots,
):
    n_dev = lax.axis_size(AXES)
    leaf_dev, width = child_m2l.shape
    slot_table = obs_offset.shape[0]
    points = obs_offset.shape[2]
    capacity = slot_table // n_dev
    block_rows = 4 * capacity + 8
    lanes = -(-width // points) * points
    my_index = lax.axis_index(AXES)
    vmem, smem = pl.BlockSpec(memory_space=pltpu.VMEM), pl.BlockSpec(memory_space=pltpu.SMEM)
    params = pltpu.CompilerParams(vmem_limit_bytes=VMEM_LIMIT)

    mine = lax.dynamic_slice_in_dim(obs_owner, my_index * leaf_dev, leaf_dev)
    counts = jnp.sum((obs_owner.reshape(n_dev, leaf_dev) == my_index).astype(jnp.int32), axis=1)
    live = (jnp.arange(capacity, dtype=jnp.int32)[None, :] < counts[:, None]).astype(jnp.int32).reshape(slot_table)

    leaf_at = jnp.arange(leaf_dev, dtype=jnp.int32)
    same = (mine[:, None] == mine[None, :]) & (leaf_at[None, :] < leaf_at[:, None])
    rank = jnp.sum(same.astype(jnp.int32), axis=1)
    rim_rows = from_behind(parent_local[parent_local.shape[0] - RIM :], AXES, 1)
    packed = pl.pallas_call(
        functools.partial(pack_sources, capacity),
        out_shape=jax.ShapeDtypeStruct((n_dev * block_rows, points), F32),
        in_specs=[smem, smem, smem, vmem, vmem],
        out_specs=vmem,
        compiler_params=params,
        name="pack_sources",
    )(mine, rank, leaf_center.T.reshape(-1), src_coords.transpose(1, 0, 2), src_charge)
    packed, rim_rows = lax.optimization_barrier((packed, rim_rows))
    recv = lax.all_to_all(
        packed.reshape(n_dev, block_rows, points), AXES, split_axis=0, concat_axis=0, tiled=True
    ).reshape(n_dev * block_rows, points)

    parents = jnp.concatenate([rim_rows, parent_local], axis=0)
    moved = jnp.einsum("pr,oqr->opq", parents, l2l_ops, precision=lax.Precision.HIGHEST)
    stacked = moved.reshape(8 * parents.shape[0], width)
    leaf_local, packed_dens = pl.pallas_call(
        route_leaves,
        out_shape=(
            jax.ShapeDtypeStruct((leaf_dev, width), F32),
            jax.ShapeDtypeStruct((slot_table, lanes), F32),
        ),
        in_specs=[smem, smem, vmem, vmem],
        out_specs=(vmem, vmem),
        compiler_params=params,
        name="route_leaves",
    )(child_octant * parents.shape[0] + parent_slot, mine * capacity + rank, child_m2l, stacked)
    dens = lax.all_to_all(
        packed_dens.reshape(n_dev, capacity, lanes), AXES, split_axis=0, concat_axis=0, tiled=True
    ).reshape(slot_table, lanes)

    obs = obs_offset.transpose(1, 0, 2)
    pairs = slot_table * near_slots.shape[1] * points * points
    near = pl.pallas_call(
        functools.partial(near_kernel, capacity, n_dev),
        out_shape=jax.ShapeDtypeStruct((slot_table, points), F32),
        in_specs=[smem, vmem, vmem],
        out_specs=vmem,
        scratch_shapes=[
            pltpu.VMEM((slot_table, FEATS, points), BF16),
            pltpu.VMEM((slot_table, FEATS, points), BF16),
            pltpu.VMEM((slot_table, points), F32),
            pltpu.VMEM((GROUP * FEATS, points), F32),
            pltpu.VMEM((GROUP * FEATS, points), F32),
            pltpu.VMEM((GROUP, points, FEATS), BF16),
            pltpu.VMEM((GROUP, points, FEATS), BF16),
            pltpu.VMEM((GROUP, points, points), F32),
            pltpu.VMEM((GROUP, points, points), F32),
        ],
        compiler_params=params,
        cost_estimate=pl.CostEstimate(flops=70 * pairs, bytes_accessed=5 * 10**6, transcendentals=pairs),
        name="near_field",
    )(near_slots.reshape(-1), recv, obs)
    potential = pl.pallas_call(
        far_kernel,
        out_shape=jax.ShapeDtypeStruct((slot_table, points), F32),
        in_specs=[vmem, vmem, vmem, vmem],
        out_specs=vmem,
        scratch_shapes=[
            pltpu.VMEM((lanes, points), F32),
            pltpu.VMEM((3, points, points), F32),
            pltpu.VMEM((points, points), F32),
        ],
        compiler_params=params,
        cost_estimate=pl.CostEstimate(flops=10**10, bytes_accessed=5 * 10**6, transcendentals=10**7),
        name="far_field",
    )(dens, obs, near, live.reshape(slot_table // points, points))
    return (leaf_local, potential)


def solution(mesh):
    placed = (
        P(AXES, None),
        P(AXES),
        P(AXES),
        P(AXES, None),
        P(),
        P(AXES, None),
        P(AXES, None, None),
        P(AXES, None),
        P(),
        P(AXES, None, None),
        P(AXES, None),
    )
    return jax.shard_map(
        on_device,
        mesh=mesh,
        in_specs=placed,
        out_specs=(P(AXES, None), P(AXES, None)),
        check_vma=False,
    )
```

```python
import functools
import math

import jax
import jax.numpy as jnp
import numpy as np
from jax import lax
from jax.experimental import pallas as pl
from jax.experimental.pallas import tpu as pltpu
from jax.sharding import PartitionSpec as P

ORDER = 8
RIM = 16
RADIUS = 2.95
HALF_WIDTH = 0.5
SOFT_SQ = 0.0025
FOUR_PI = 4.0 * math.pi
AXES = ("grp", "dom")
FEATS = 32
GROUP = 8
VMEM_LIMIT = 50 * 1024 * 1024

F32 = jnp.float32
BF16 = jnp.bfloat16


def from_behind(block, axis, distance):
    devices = range(lax.axis_size(axis))
    route = [(i - distance, i) for i in devices if i - distance in devices]
    return lax.ppermute(block, axis, route)


def surface_grid():
    axis = (np.linspace(-1.0, 1.0, ORDER) * RADIUS).astype(np.float32)
    ends = (0, ORDER - 1)
    points = [
        (i, j, k)
        for i in range(ORDER)
        for j in range(ORDER)
        for k in range(ORDER)
        if i in ends or j in ends or k in ends
    ]
    return [float(value) for value in axis], points


def split(value):
    high = value.astype(BF16).astype(F32)
    rest = value - high
    mid = rest.astype(BF16).astype(F32)
    return high, mid, rest - mid


def sub_of(shape):
    return lax.broadcasted_iota(jnp.int32, shape, 0)


def stack_rows(x, y, z):
    place = sub_of((GROUP, x.shape[1])) % 4
    return jnp.where(place == 0, x, jnp.where(place == 1, y, z))


def norm_rows(points, extra):
    place = sub_of(points.shape) % 4
    squares = jnp.where(place == 3, extra, points * points)
    squares = squares + pltpu.roll(squares, 1, 0)
    return squares + pltpu.roll(squares, 2, 0)


def put_rows(pair, third, last):
    sub = sub_of(pair[0].shape)
    block = jnp.where(sub < 4, pair[0], pair[1])
    return jnp.where(sub == 3, third, jnp.where(sub == 7, last, block))


def source_pieces(points):
    high, mid, low = split(points)
    n_high, n_mid, n_low = split(norm_rows(points, 0.0))
    return jnp.concatenate(
        [
            put_rows((high, high), 1.0, 1.0),
            put_rows((high, mid), 1.0, n_high),
            put_rows((mid, low), n_mid, n_low),
            jnp.zeros_like(points),
        ],
        axis=0,
    ).astype(BF16)


def target_pieces(points):
    high, mid, low = split(-2.0 * points)
    n_high, n_mid, n_low = split(norm_rows(points, SOFT_SQ))
    return jnp.concatenate(
        [
            put_rows((high, mid), n_high, n_mid),
            put_rows((low, high), n_low, 1.0),
            put_rows((mid, high), 1.0, 1.0),
            jnp.zeros_like(points),
        ],
        axis=0,
    ).astype(BF16)


def lane_sums(block):
    high = block.astype(BF16)
    low = (block - high.astype(F32)).astype(BF16)
    ones = jnp.ones((GROUP, 2 * block.shape[1]), BF16)
    pieces = jnp.concatenate([high, low], axis=1)
    return lax.dot_general(ones, pieces, (((1,), (1,)), ((), ())), preferred_element_type=F32)


def pack_sources(capacity, owner_ref, rank_ref, center_ref, coords_ref, charge_ref, first_ref, second_ref, packed_ref):
    rows = 2 * capacity + 8
    leaves, points = charge_ref.shape
    n_dev = first_ref.shape[0] // rows
    lane = lax.broadcasted_iota(jnp.int32, (GROUP, points), 1)
    sub = sub_of((GROUP, points)) % 4

    def step(j, carry):
        owner, rank = owner_ref[j], rank_ref[j]
        base = owner * 4 * capacity + rank
        for c in range(3):
            packed_ref[pl.ds(base + c * capacity, 1), :] = coords_ref[c, pl.ds(j, 1), :]
        packed_ref[pl.ds(base + 3 * capacity, 1), :] = charge_ref[pl.ds(j, 1), :]
        place = pl.ds(pl.multiple_of(owner * rows + 2 * capacity, GROUP), GROUP)
        value = jnp.where(
            sub == 0,
            center_ref[j],
            jnp.where(sub == 1, center_ref[leaves + j], center_ref[2 * leaves + j]),
        )
        first_ref[place, :] = jnp.where(lane == rank, value, first_ref[place, :])
        return carry

    lax.fori_loop(0, leaves, step, 0, unroll=4)

    def halves(d, carry):
        for pair in range(2):
            for g in range(0, capacity, GROUP):
                at = d * 4 * capacity + 2 * pair * capacity + g
                left = packed_ref[pl.ds(pl.multiple_of(at, GROUP), GROUP), :]
                right = packed_ref[pl.ds(pl.multiple_of(at + capacity, GROUP), GROUP), :]
                place = pl.ds(pl.multiple_of(d * rows + pair * capacity + g, GROUP), GROUP)
                first_ref[place, :] = jnp.where(
                    lane < points // 2, left, pltpu.roll(right, points // 2, 1)
                )
                place = pl.ds(pl.multiple_of((2 * d + pair) * capacity + g, GROUP), GROUP)
                second_ref[place, :] = jnp.where(
                    lane < points // 2, pltpu.roll(left, points // 2, 1), right
                )
        return carry

    lax.fori_loop(0, n_dev, halves, 0)


def route_leaves(index_ref, dest_ref, m2l_ref, moved_ref, leaf_ref, out_ref):
    def step(j, carry):
        row = m2l_ref[pl.ds(j, 1), :] + moved_ref[pl.ds(index_ref[j], 1), :]
        leaf_ref[pl.ds(j, 1), :] = row
        out_ref[pl.ds(dest_ref[j], 1), : row.shape[1]] = row
        return carry

    lax.fori_loop(0, m2l_ref.shape[0], step, 0, unroll=4)


def near_kernel(
    capacity,
    n_dev,
    rows,
    center_rows,
    slots_ref,
    recv_ref,
    center_ref,
    obs_ref,
    out_ref,
    source_ref,
    charge_ref,
    stage_ref,
    left_a,
    left_b,
    total_a,
    total_b,
):
    points = out_ref.shape[1]
    half = points // 2
    blocks = out_ref.shape[0] // GROUP
    sub = sub_of((GROUP, points))
    low = lax.broadcasted_iota(jnp.int32, (GROUP, points), 1) < half
    low_row = lax.broadcasted_iota(jnp.int32, (1, points), 1) < half
    low_block = lax.broadcasted_iota(jnp.int32, (FEATS, points), 1).astype(F32).astype(BF16) < half

    def both(value):
        turned = pltpu.roll(value, half, 1)
        return jnp.where(low, value, turned), jnp.where(low, turned, value)

    def prepare(s, carry):
        for g in range(0, capacity, GROUP):
            slot = pl.multiple_of(s * capacity + g, GROUP)
            at = pl.multiple_of(s * rows + g, GROUP)
            x, y = both(recv_ref[pl.ds(at, GROUP), :])
            z, charge = both(recv_ref[pl.ds(at + capacity, GROUP), :])
            charge_ref[pl.ds(slot, GROUP), :] = charge
            for c, value in enumerate((x, y, z)):
                stage_ref[pl.ds(3 * g + c * GROUP, GROUP), :] = value - 1.0
            for u in range(GROUP):
                parts = [stage_ref[pl.ds(3 * g + c * GROUP + u, 1), :] for c in range(3)]
                source_ref[slot + u] = source_pieces(stack_rows(*parts))
        return carry

    lax.fori_loop(0, n_dev, prepare, 0)

    def block_centers(block):
        dev = block * GROUP // capacity
        place = pl.ds(pl.multiple_of(dev * center_rows + 2 * capacity, GROUP), GROUP)
        column = block * GROUP - dev * capacity
        return pltpu.roll(center_ref[place, :], lax.rem(points - column, points), 1)

    def turn(block, centers, u, left_ref):
        parts = [obs_ref[c, pl.ds(block * GROUP + u, 1), :] for c in range(3)]
        targets = (centers[:, u : u + 1] - 1.0) + HALF_WIDTH * stack_rows(*parts)
        left_ref[u] = target_pieces(targets).T

    def pair_work(block, u, left_ref, total_ref):
        left = left_ref[u]
        at = (block * GROUP + u) * GROUP
        total = None
        for p in range(2):
            index = [slots_ref[at + 4 * p + n] for n in range(4)]
            sources, charges = [], []
            for n in (0, 2):
                one, two = index[n], index[n + 1]
                sources.append(jnp.where(low_block, source_ref[one], source_ref[two]))
                charges.append(
                    jnp.where(low_row, charge_ref[pl.ds(one, 1), :], charge_ref[pl.ds(two, 1), :])
                )
            right = jnp.concatenate(sources, axis=1)
            inverse = lax.rsqrt(jnp.dot(left, right, preferred_element_type=F32))
            part = inverse[:, :points] * charges[0] + inverse[:, points:] * charges[1]
            total = part if total is None else total + part
        total_ref[u] = total

    def half_step(before, block, after, left_now, left_next, total_before, total_now):
        sums = None
        centers = block_centers(after)
        for u in range(GROUP):
            turn(after, centers, u, left_next)
            pair_work(block, u, left_now, total_now)
            part = lane_sums(total_before[u])
            sums = part if sums is None else jnp.where(sub == u, part, sums)
        out_ref[pl.ds(pl.multiple_of(before * GROUP, GROUP), GROUP), :] = sums

    centers = block_centers(0)
    for u in range(GROUP):
        turn(0, centers, u, left_a)
    total_b[...] = jnp.zeros_like(total_b)

    def step(i, carry):
        one, two = 2 * i, 2 * i + 1
        half_step(jnp.maximum(one - 1, 0), one, two, left_a, left_b, total_b, total_a)
        half_step(one, two, jnp.minimum(two + 1, blocks - 1), left_b, left_a, total_a, total_b)
        return carry

    lax.fori_loop(0, blocks // 2, step, 0)
    sums = None
    for u in range(GROUP):
        part = lane_sums(total_b[u])
        sums = part if sums is None else jnp.where(sub == u, part, sums)
    out_ref[pl.ds((blocks - 1) * GROUP, GROUP), :] = sums


def far_kernel(dens_ref, obs_ref, near_ref, near_too_ref, live_ref, out_ref, turned_ref, point_ref, far_ref):
    axis, surface = surface_grid()
    number = {point: q for q, point in enumerate(surface)}
    side = out_ref.shape[1]

    def tile(t, carry):
        first = pl.multiple_of(t * side, side)
        for column in range(0, dens_ref.shape[1], side):
            turned_ref[pl.ds(column, side), :] = dens_ref[pl.ds(first, side), pl.ds(column, side)].T
        for c in range(3):
            point_ref[c] = obs_ref[c, pl.ds(first, side), :].T

        def points(b, carry):
            place = pl.ds(pl.multiple_of(b * GROUP, GROUP), GROUP)
            squares = []
            for c in range(3):
                value = point_ref[c, place, :]
                squares.append([(value - at) * (value - at) for at in axis])
            totals = [jnp.zeros((GROUP, side), F32) for _ in range(4)]
            turn = 0
            for j in range(ORDER):
                for k in range(ORDER):
                    partial = squares[1][j] + squares[2][k]
                    for i in range(ORDER):
                        q = number.get((i, j, k))
                        if q is None:
                            continue
                        inverse = lax.rsqrt(squares[0][i] + partial)
                        totals[turn] = totals[turn] + inverse * turned_ref[pl.ds(q, 1), :]
                        turn = (turn + 1) % 4
            far_ref[place, :] = (totals[0] + totals[1]) + (totals[2] + totals[3])
            return carry

        lax.fori_loop(0, side // GROUP, points, 0)
        near = (near_ref[pl.ds(first, side), :] + near_too_ref[pl.ds(first, side), :]).T
        total = far_ref[...] * (1.0 / (FOUR_PI * HALF_WIDTH)) + near * (1.0 / FOUR_PI)
        total = jnp.where(live_ref[pl.ds(t, 1), :] > 0, total, 0.0)
        out_ref[pl.ds(first, side), :] = total.T
        return carry

    lax.fori_loop(0, out_ref.shape[0] // side, tile, 0)


def on_device(
    parent_local,
    parent_slot,
    child_octant,
    child_m2l,
    l2l_ops,
    leaf_center,
    src_coords,
    src_charge,
    obs_owner,
    obs_offset,
    near_slots,
):
    n_dev = lax.axis_size(AXES)
    leaf_dev, width = child_m2l.shape
    slot_table = obs_offset.shape[0]
    points = obs_offset.shape[2]
    capacity = slot_table // n_dev
    block_rows = 2 * capacity + 8
    lanes = -(-width // points) * points
    my_index = lax.axis_index(AXES)
    vmem, smem = pl.BlockSpec(memory_space=pltpu.VMEM), pl.BlockSpec(memory_space=pltpu.SMEM)
    params = pltpu.CompilerParams(vmem_limit_bytes=VMEM_LIMIT)

    mine = lax.dynamic_slice_in_dim(obs_owner, my_index * leaf_dev, leaf_dev)
    counts = jnp.sum((obs_owner.reshape(n_dev, leaf_dev) == my_index).astype(jnp.int32), axis=1)
    live = (jnp.arange(capacity, dtype=jnp.int32)[None, :] < counts[:, None]).astype(jnp.int32).reshape(slot_table)

    leaf_at = jnp.arange(leaf_dev, dtype=jnp.int32)
    same = (mine[:, None] == mine[None, :]) & (leaf_at[None, :] < leaf_at[:, None])
    rank = jnp.sum(same.astype(jnp.int32), axis=1)
    rim_rows = from_behind(parent_local[parent_local.shape[0] - RIM :], AXES, 1)
    rim_rows = from_behind(parent_local[parent_local.shape[0] - RIM :], AXES, 1)
    first_part, second_part = pl.pallas_call(
        functools.partial(pack_sources, capacity),
        out_shape=(
            jax.ShapeDtypeStruct((n_dev * block_rows, points), F32),
            jax.ShapeDtypeStruct((slot_table * 2, points), F32),
        ),
        in_specs=[smem, smem, smem, vmem, vmem],
        out_specs=(vmem, vmem),
        scratch_shapes=[pltpu.VMEM((slot_table * 4, points), F32)],
        compiler_params=params,
        name="pack_sources",
    )(mine, rank, leaf_center.T.reshape(-1), src_coords.transpose(1, 0, 2), src_charge)
    first_part, rim_rows = lax.optimization_barrier((first_part, rim_rows))

    def exchange(packed):
        blocks = packed.reshape(n_dev, -1, packed.shape[1])
        got = lax.all_to_all(blocks, AXES, split_axis=0, concat_axis=0, tiled=True)
        return got.reshape(packed.shape)

    first_recv = exchange(first_part)
    second_part, first_recv = lax.optimization_barrier((second_part, first_recv))
    second_recv = exchange(second_part)
    parents = jnp.concatenate([rim_rows, parent_local], axis=0)
    moved = jnp.einsum("pr,oqr->opq", parents, l2l_ops, precision=lax.Precision.HIGHEST)
    stacked = moved.reshape(8 * parents.shape[0], width)
    leaf_local, packed_dens = pl.pallas_call(
        route_leaves,
        out_shape=(
            jax.ShapeDtypeStruct((leaf_dev, width), F32),
            jax.ShapeDtypeStruct((slot_table, lanes), F32),
        ),
        in_specs=[smem, smem, vmem, vmem],
        out_specs=(vmem, vmem),
        compiler_params=params,
        name="route_leaves",
    )(child_octant * parents.shape[0] + parent_slot, mine * capacity + rank, child_m2l, stacked)
    packed_dens, second_recv = lax.optimization_barrier((packed_dens, second_recv))
    dens = exchange(packed_dens)

    obs = obs_offset.transpose(1, 0, 2)
    slots = near_slots.reshape(-1)
    pairs = slot_table * near_slots.shape[1] * points * points // 2

    def near_part(recv, name):
        return pl.pallas_call(
            functools.partial(near_kernel, capacity, n_dev, recv.shape[0] // n_dev, block_rows),
            out_shape=jax.ShapeDtypeStruct((slot_table, points), F32),
            in_specs=[smem, vmem, vmem, vmem],
            out_specs=vmem,
            scratch_shapes=[
                pltpu.VMEM((slot_table, FEATS, points), BF16),
                pltpu.VMEM((slot_table, points), F32),
                pltpu.VMEM((3 * capacity, points), F32),
                pltpu.VMEM((GROUP, points, FEATS), BF16),
                pltpu.VMEM((GROUP, points, FEATS), BF16),
                pltpu.VMEM((GROUP, points, points), F32),
                pltpu.VMEM((GROUP, points, points), F32),
            ],
            compiler_params=params,
            cost_estimate=pl.CostEstimate(
                flops=70 * pairs, bytes_accessed=5 * 10**6, transcendentals=pairs
            ),
            name=name,
        )(slots, recv, first_recv, obs)

    near = near_part(first_recv, "near_first")
    near_too = near_part(second_recv, "near_second")
    potential = pl.pallas_call(
        far_kernel,
        out_shape=jax.ShapeDtypeStruct((slot_table, points), F32),
        in_specs=[vmem, vmem, vmem, vmem, vmem],
        out_specs=vmem,
        scratch_shapes=[
            pltpu.VMEM((lanes, points), F32),
            pltpu.VMEM((3, points, points), F32),
            pltpu.VMEM((points, points), F32),
        ],
        compiler_params=params,
        cost_estimate=pl.CostEstimate(flops=10**10, bytes_accessed=5 * 10**6, transcendentals=10**7),
        name="far_field",
    )(dens, obs, near, near_too, live.reshape(slot_table // points, points))
    return (leaf_local, potential)


def solution(mesh):
    placed = (
        P(AXES, None),
        P(AXES),
        P(AXES),
        P(AXES, None),
        P(),
        P(AXES, None),
        P(AXES, None, None),
        P(AXES, None),
        P(),
        P(AXES, None, None),
        P(AXES, None),
    )
    return jax.shard_map(
        on_device,
        mesh=mesh,
        in_specs=placed,
        out_specs=(P(AXES, None), P(AXES, None)),
        check_vma=False,
    )
```

```python
import functools
import math

import jax
import jax.numpy as jnp
import numpy as np
from jax import lax
from jax.experimental import pallas as pl
from jax.experimental.pallas import tpu as pltpu
from jax.sharding import PartitionSpec as P

ORDER = 8
RIM = 16
RADIUS = 2.95
HALF_WIDTH = 0.5
SOFT_SQ = 0.0025
FOUR_PI = 4.0 * math.pi
AXES = ("grp", "dom")
FEATS = 32
GROUP = 8
VMEM_LIMIT = 32 * 1024 * 1024

F32 = jnp.float32
BF16 = jnp.bfloat16


def from_behind(block, axis, distance):
    devices = range(lax.axis_size(axis))
    route = [(i - distance, i) for i in devices if i - distance in devices]
    return lax.ppermute(block, axis, route)


def surface_grid():
    axis = (np.linspace(-1.0, 1.0, ORDER) * RADIUS).astype(np.float32)
    ends = (0, ORDER - 1)
    points = [
        (i, j, k)
        for i in range(ORDER)
        for j in range(ORDER)
        for k in range(ORDER)
        if i in ends or j in ends or k in ends
    ]
    return [float(value) for value in axis], points


def split(value):
    high = value.astype(BF16).astype(F32)
    rest = value - high
    mid = rest.astype(BF16).astype(F32)
    return high, mid, rest - mid


def point_rows(coords, extra, is_target):
    norm = coords[0] * coords[0] + coords[1] * coords[1] + coords[2] * coords[2] + extra
    ones = jnp.ones_like(norm)
    rows = []
    for value in coords:
        high, mid, low = split(-2.0 * value if is_target else value)
        rows += [high, mid, low, high, mid, high] if is_target else [high, high, high, mid, mid, low]
    norms = list(split(norm))
    rows += norms + [ones] * 3 if is_target else [ones] * 3 + norms
    return rows


def store_feats(stage_ref, out_ref, base, rows):
    for f, row in enumerate(rows):
        stage_ref[pl.ds(f, GROUP, stride=FEATS), :] = row
    out_ref[pl.ds(base, GROUP)] = stage_ref[...].reshape(GROUP, FEATS, row.shape[1]).astype(BF16)


def clear_stage(stage_ref):
    stage_ref[...] = jnp.zeros_like(stage_ref)


def lane_sums(block):
    high = block.astype(BF16)
    low = (block - high.astype(F32)).astype(BF16)
    ones = jnp.ones((GROUP, 2 * block.shape[1]), BF16)
    pieces = jnp.concatenate([high, low], axis=1)
    return lax.dot_general(ones, pieces, (((1,), (1,)), ((), ())), preferred_element_type=F32)


def pack_sources(capacity, owner_ref, rank_ref, coords_ref, charge_ref, out_ref):
    def step(j, carry):
        at = owner_ref[j] * 4 * capacity + rank_ref[j]
        for c in range(3):
            out_ref[pl.ds(at + c * capacity, 1), :] = coords_ref[c, pl.ds(j, 1), :]
        out_ref[pl.ds(at + 3 * capacity, 1), :] = charge_ref[pl.ds(j, 1), :]
        return carry

    lax.fori_loop(0, charge_ref.shape[0], step, 0, unroll=8)


def target_kernel(points_ref, out_ref, stage_ref):
    clear_stage(stage_ref)

    def prepare(g, carry):
        slot = pl.multiple_of(g * GROUP, GROUP)
        coords = [points_ref[c, pl.ds(slot, GROUP), :] for c in range(3)]
        store_feats(stage_ref, out_ref, slot, point_rows(coords, SOFT_SQ, True))
        return carry

    lax.fori_loop(0, out_ref.shape[0] // GROUP, prepare, 0, unroll=2)


def route_leaves(index_ref, dest_ref, m2l_ref, moved_ref, leaf_ref, out_ref):
    def step(j, carry):
        row = m2l_ref[pl.ds(j, 1), :] + moved_ref[pl.ds(index_ref[j], 1), :]
        leaf_ref[pl.ds(j, 1), :] = row
        out_ref[pl.ds(dest_ref[j], 1), : row.shape[1]] = row
        return carry

    lax.fori_loop(0, m2l_ref.shape[0], step, 0, unroll=4)


def near_kernel(
    capacity,
    n_dev,
    slots_ref,
    recv_ref,
    target_ref,
    out_ref,
    turned_ref,
    source_ref,
    charge_ref,
    stage_ref,
    left_a,
    left_b,
    total_a,
    total_b,
):
    blocks = out_ref.shape[0] // GROUP
    side = out_ref.shape[1]
    lane = lax.broadcasted_iota(jnp.int32, (side, side), 1)
    sub = lax.broadcasted_iota(jnp.int32, (GROUP, side), 0)
    clear_stage(stage_ref)
    turned_ref[...] = jnp.zeros_like(turned_ref)

    def prepare(s, carry):
        for g in range(0, capacity, GROUP):
            slot = pl.multiple_of(s * capacity + g, GROUP)
            at = pl.multiple_of(s * 4 * capacity + g, GROUP)
            coords = [recv_ref[pl.ds(at + c * capacity, GROUP), :] - 1.0 for c in range(3)]
            store_feats(stage_ref, source_ref, slot, point_rows(coords, 0.0, False))
            charge_ref[pl.ds(slot, GROUP), :] = recv_ref[pl.ds(at + 3 * capacity, GROUP), :]
        return carry

    lax.fori_loop(0, n_dev, prepare, 0)

    def turn(block, u, left_ref):
        left_ref[u] = target_ref[block * GROUP + u].T

    def pair_work(block, u, left_ref, total_ref):
        left = left_ref[u]
        at = (block * GROUP + u) * GROUP
        total = None
        for p in range(4):
            first, second = slots_ref[at + 2 * p], slots_ref[at + 2 * p + 1]
            right = jnp.concatenate([source_ref[first], source_ref[second]], axis=1)
            inverse = lax.rsqrt(jnp.dot(left, right, preferred_element_type=F32))
            part = (
                inverse[:, :128] * charge_ref[pl.ds(first, 1), :]
                + inverse[:, 128:] * charge_ref[pl.ds(second, 1), :]
            )
            total = part if total is None else total + part
        total_ref[u] = total

    def put_sums(block, total_ref):
        column = lax.rem(block * GROUP, side)
        place = pl.ds(pl.multiple_of(block * GROUP - column, side), side)
        rows, columns = jnp.zeros((GROUP, side), F32), turned_ref[place, :]

        def add_row(sums, u):
            rows, columns = sums
            if u < GROUP // 2:
                return jnp.where(sub == u, lane_sums(total_ref[u]), rows), columns
            row = jnp.sum(total_ref[u], axis=1, keepdims=True)
            return rows, jnp.where(lane == column + u, row, columns)

        def finish(sums):
            out_ref[pl.ds(pl.multiple_of(block * GROUP, GROUP), GROUP), :] = sums[0]
            turned_ref[place, :] = sums[1]

        return (rows, columns), add_row, finish

    def half(before, block, after, left_now, left_next, total_before, total_now):
        sums, add_row, finish = put_sums(before, total_before)
        for u in range(GROUP):
            turn(after, u, left_next)
            pair_work(block, u, left_now, total_now)
            sums = add_row(sums, (u % 2) * (GROUP // 2) + u // 2)
        finish(sums)

    for u in range(GROUP):
        turn(0, u, left_a)
    total_b[...] = jnp.zeros_like(total_b)

    def step(i, carry):
        one, two = 2 * i, 2 * i + 1
        half(jnp.maximum(one - 1, 0), one, two, left_a, left_b, total_b, total_a)
        half(one, two, jnp.minimum(two + 1, blocks - 1), left_b, left_a, total_a, total_b)
        return carry

    lax.fori_loop(0, blocks // 2, step, 0)
    sums, add_row, finish = put_sums(blocks - 1, total_b)
    for u in range(GROUP):
        sums = add_row(sums, u)
    finish(sums)


def far_kernel(dens_ref, obs_ref, near_ref, turned_near_ref, live_ref, out_ref, turned_ref, far_ref):
    axis, surface = surface_grid()
    number = {point: q for q, point in enumerate(surface)}
    side = out_ref.shape[1]

    def tile(t, carry):
        first = pl.multiple_of(t * side, side)
        for column in range(0, dens_ref.shape[1], side):
            turned_ref[pl.ds(column, side), :] = dens_ref[pl.ds(first, side), pl.ds(column, side)].T

        def points(b, carry):
            place = pl.ds(pl.multiple_of(b * GROUP, GROUP), GROUP)
            squares = []
            for c in range(3):
                value = obs_ref[c, place, pl.ds(first, side)]
                squares.append([(value - at) * (value - at) for at in axis])
            totals = [jnp.zeros((GROUP, side), F32) for _ in range(4)]
            turn = 0
            for j in range(ORDER):
                for k in range(ORDER):
                    partial = squares[1][j] + squares[2][k]
                    for i in range(ORDER):
                        q = number.get((i, j, k))
                        if q is None:
                            continue
                        inverse = lax.rsqrt(squares[0][i] + partial)
                        totals[turn] = totals[turn] + inverse * turned_ref[pl.ds(q, 1), :]
                        turn = (turn + 1) % 4
            far_ref[place, :] = (totals[0] + totals[1]) + (totals[2] + totals[3])
            return carry

        lax.fori_loop(0, side // GROUP, points, 0)
        near = near_ref[pl.ds(first, side), :].T + turned_near_ref[pl.ds(first, side), :]
        total = far_ref[...] * (1.0 / (FOUR_PI * HALF_WIDTH)) + near * (1.0 / FOUR_PI)
        total = jnp.where(live_ref[pl.ds(t, 1), :] > 0, total, 0.0)
        out_ref[pl.ds(first, side), :] = total.T
        return carry

    lax.fori_loop(0, out_ref.shape[0] // side, tile, 0)


def on_device(
    parent_local,
    parent_slot,
    child_octant,
    child_m2l,
    l2l_ops,
    leaf_center,
    src_coords,
    src_charge,
    obs_owner,
    obs_offset,
    near_slots,
):
    n_dev = lax.axis_size(AXES)
    leaf_dev, width = child_m2l.shape
    slot_table = obs_offset.shape[0]
    points = obs_offset.shape[2]
    capacity = slot_table // n_dev
    block_rows = 4 * capacity
    lanes = -(-width // points) * points
    my_index = lax.axis_index(AXES)
    vmem, smem = pl.BlockSpec(memory_space=pltpu.VMEM), pl.BlockSpec(memory_space=pltpu.SMEM)
    params = pltpu.CompilerParams(vmem_limit_bytes=VMEM_LIMIT)

    mine = lax.dynamic_slice_in_dim(obs_owner, my_index * leaf_dev, leaf_dev)
    center_rows = leaf_center.T.reshape(3 * leaf_dev // points, points)
    all_centers = lax.all_gather(center_rows, AXES, axis=0, tiled=True).reshape(n_dev, 3, leaf_dev)
    leaf_at = jnp.arange(leaf_dev, dtype=jnp.int32)
    same = (mine[:, None] == mine[None, :]) & (leaf_at[None, :] < leaf_at[:, None])
    rank = jnp.sum(same.astype(jnp.int32), axis=1)
    rim_rows = from_behind(parent_local[parent_local.shape[0] - RIM :], AXES, 1)
    packed = pl.pallas_call(
        functools.partial(pack_sources, capacity),
        out_shape=jax.ShapeDtypeStruct((n_dev * block_rows, points), F32),
        in_specs=[smem, smem, vmem, vmem],
        out_specs=vmem,
        compiler_params=params,
        name="pack_sources",
    )(mine, rank, src_coords.transpose(1, 0, 2), src_charge)
    packed, rim_rows, obs_owner, obs_offset, near_slots, child_m2l = lax.optimization_barrier(
        (packed, rim_rows, obs_owner, obs_offset, near_slots, child_m2l)
    )
    recv = lax.all_to_all(
        packed.reshape(n_dev, block_rows, points), AXES, split_axis=0, concat_axis=0, tiled=True
    ).reshape(n_dev * block_rows, points)

    to_me = (obs_owner.reshape(n_dev, leaf_dev) == my_index).astype(jnp.int32)
    order = jnp.cumsum(to_me, axis=1) * to_me
    counts = jnp.sum(to_me, axis=1)
    slot_at = jnp.arange(capacity, dtype=jnp.int32)
    live = (slot_at[None, :] < counts[:, None]).astype(jnp.int32).reshape(slot_table // points, points)

    chosen = order[:, None, :] == slot_at[None, :, None] + 1
    centers = jnp.stack(
        [
            jnp.sum(jnp.where(chosen, all_centers[:, c, None, :], 0.0), axis=2).reshape(slot_table)
            for c in range(3)
        ]
    )
    obs = obs_offset.transpose(1, 0, 2)
    turned_obs = obs.transpose(0, 2, 1)
    slots = near_slots.reshape(-1)
    target_points = (centers - 1.0)[:, :, None] + HALF_WIDTH * obs

    parents = jnp.concatenate([rim_rows, parent_local], axis=0)
    moved = jnp.einsum("pr,oqr->opq", parents, l2l_ops, precision=lax.Precision.HIGHEST)
    stacked = moved.reshape(8 * parents.shape[0], width)
    leaf_local, packed_dens = pl.pallas_call(
        route_leaves,
        out_shape=(
            jax.ShapeDtypeStruct((leaf_dev, width), F32),
            jax.ShapeDtypeStruct((slot_table, lanes), F32),
        ),
        in_specs=[smem, smem, vmem, vmem],
        out_specs=(vmem, vmem),
        compiler_params=params,
        name="route_leaves",
    )(child_octant * parents.shape[0] + parent_slot, mine * capacity + rank, child_m2l, stacked)
    targets = pl.pallas_call(
        target_kernel,
        out_shape=jax.ShapeDtypeStruct((slot_table, FEATS, points), BF16),
        in_specs=[vmem],
        out_specs=vmem,
        scratch_shapes=[pltpu.VMEM((GROUP * FEATS, points), F32)],
        compiler_params=params,
        name="target_pieces",
    )(target_points)
    packed_dens, targets, slots, live, turned_obs = lax.optimization_barrier(
        (packed_dens, targets, slots, live, turned_obs)
    )
    dens = lax.all_to_all(
        packed_dens.reshape(n_dev, capacity, lanes), AXES, split_axis=0, concat_axis=0, tiled=True
    ).reshape(slot_table, lanes)

    pairs = slot_table * near_slots.shape[1] * points * points
    near, turned_near = pl.pallas_call(
        functools.partial(near_kernel, capacity, n_dev),
        out_shape=(
            jax.ShapeDtypeStruct((slot_table, points), F32),
            jax.ShapeDtypeStruct((slot_table, points), F32),
        ),
        in_specs=[smem, vmem, vmem],
        out_specs=(vmem, vmem),
        scratch_shapes=[
            pltpu.VMEM((slot_table, FEATS, points), BF16),
            pltpu.VMEM((slot_table, points), F32),
            pltpu.VMEM((GROUP * FEATS, points), F32),
            pltpu.VMEM((GROUP, points, FEATS), BF16),
            pltpu.VMEM((GROUP, points, FEATS), BF16),
            pltpu.VMEM((GROUP, points, points), F32),
            pltpu.VMEM((GROUP, points, points), F32),
        ],
        compiler_params=params,
        cost_estimate=pl.CostEstimate(flops=70 * pairs, bytes_accessed=5 * 10**6, transcendentals=pairs),
        name="near_field",
    )(slots, recv, targets)
    potential = pl.pallas_call(
        far_kernel,
        out_shape=jax.ShapeDtypeStruct((slot_table, points), F32),
        in_specs=[vmem, vmem, vmem, vmem, vmem],
        out_specs=vmem,
        scratch_shapes=[
            pltpu.VMEM((lanes, points), F32),
            pltpu.VMEM((points, points), F32),
        ],
        compiler_params=params,
        cost_estimate=pl.CostEstimate(flops=10**10, bytes_accessed=5 * 10**6, transcendentals=10**7),
        name="far_field",
    )(dens, turned_obs, near, turned_near, live)
    return (leaf_local, potential)


def solution(mesh):
    placed = (
        P(AXES, None),
        P(AXES),
        P(AXES),
        P(AXES, None),
        P(),
        P(AXES, None),
        P(AXES, None, None),
        P(AXES, None),
        P(),
        P(AXES, None, None),
        P(AXES, None),
    )
    return jax.shard_map(
        on_device,
        mesh=mesh,
        in_specs=placed,
        out_specs=(P(AXES, None), P(AXES, None)),
        check_vma=False,
    )
```

```python
import functools
import math

import jax
import jax.numpy as jnp
import numpy as np
from jax import lax
from jax.experimental import pallas as pl
from jax.experimental.pallas import tpu as pltpu
from jax.sharding import PartitionSpec as P

ORDER = 8
RIM = 16
RADIUS = 2.95
HALF_WIDTH = 0.5
SOFT_SQ = 0.0025
FOUR_PI = 4.0 * math.pi
AXES = ("grp", "dom")
FEATS = 32
GROUP = 8
VMEM_LIMIT = 40 * 1024 * 1024

F32 = jnp.float32
BF16 = jnp.bfloat16


def from_behind(block, axis, distance):
    devices = range(lax.axis_size(axis))
    route = [(i - distance, i) for i in devices if i - distance in devices]
    return lax.ppermute(block, axis, route)


def surface_grid():
    axis = (np.linspace(-1.0, 1.0, ORDER) * RADIUS).astype(np.float32)
    ends = (0, ORDER - 1)
    points = [
        (i, j, k)
        for i in range(ORDER)
        for j in range(ORDER)
        for k in range(ORDER)
        if i in ends or j in ends or k in ends
    ]
    return [float(value) for value in axis], points


def split(value):
    high = value.astype(BF16).astype(F32)
    rest = value - high
    mid = rest.astype(BF16).astype(F32)
    return high, mid, rest - mid


SOURCE_ORDER = ("h", "h", "h", "m", "m", "l")
TARGET_ORDER = ("h", "m", "l", "h", "m", "h")
N_PIECES = 14


def spread_matrix(order, norm_first):
    start = {"h": 0, "m": 3, "l": 6}
    pieces = [start[name] + c for c in range(3) for name in order]
    pieces += [9, 10, 11, 12, 12, 12] if norm_first else [12, 12, 12, 9, 10, 11]
    table = np.zeros((GROUP * FEATS, N_PIECES * GROUP), jnp.bfloat16)
    for u in range(GROUP):
        for f, piece in enumerate(pieces):
            table[u * FEATS + f, piece * GROUP + u] = 1.0
    return table


def piece_rows(coords, extra, scale):
    norm = coords[0] * coords[0] + coords[1] * coords[1] + coords[2] * coords[2] + extra
    parts = [split(scale * value) for value in coords]
    rows = [part[level] for level in range(3) for part in parts]
    rows += list(split(norm)) + [jnp.ones_like(norm), jnp.zeros_like(norm)]
    return jnp.concatenate(rows, axis=0).astype(BF16)


def spread(matrix_ref, blocks, out_ref, slot):
    pieces = jnp.concatenate(blocks, axis=1)
    rows = jnp.dot(matrix_ref[...], pieces, preferred_element_type=F32).astype(BF16)
    lanes = blocks[0].shape[1]
    for i in range(2):
        block = rows[:, i * lanes : (i + 1) * lanes].reshape(GROUP, FEATS, lanes)
        out_ref[pl.ds(slot + i * GROUP, GROUP)] = block


def lane_sums(block):
    high = block.astype(BF16)
    low = (block - high.astype(F32)).astype(BF16)
    ones = jnp.ones((GROUP, 2 * block.shape[1]), BF16)
    pieces = jnp.concatenate([high, low], axis=1)
    return lax.dot_general(ones, pieces, (((1,), (1,)), ((), ())), preferred_element_type=F32)


def pack_sources(capacity, owner_ref, rank_ref, center_ref, coords_ref, charge_ref, out_ref):
    rows = 4 * capacity + 8
    leaves = charge_ref.shape[0]
    lane = lax.broadcasted_iota(jnp.int32, (8, 128), 1)
    sub = lax.broadcasted_iota(jnp.int32, (8, 128), 0)
    out_ref[...] = jnp.zeros_like(out_ref)

    def step(j, carry):
        rank = rank_ref[j]
        base = owner_ref[j] * rows
        for c in range(3):
            out_ref[pl.ds(base + c * capacity + rank, 1), :] = coords_ref[c, pl.ds(j, 1), :]
        out_ref[pl.ds(base + 3 * capacity + rank, 1), :] = charge_ref[pl.ds(j, 1), :]
        place = pl.ds(pl.multiple_of(base + 4 * capacity, 8), 8)
        value = jnp.where(
            sub == 0,
            center_ref[j],
            jnp.where(sub == 1, center_ref[leaves + j], center_ref[2 * leaves + j]),
        )
        out_ref[place, :] = jnp.where(lane == rank, value, out_ref[place, :])
        return carry

    lax.fori_loop(0, leaves, step, 0, unroll=4)


def route_leaves(index_ref, dest_ref, m2l_ref, moved_ref, leaf_ref, out_ref):
    def step(j, carry):
        row = m2l_ref[pl.ds(j, 1), :] + moved_ref[pl.ds(index_ref[j], 1), :]
        leaf_ref[pl.ds(j, 1), :] = row
        out_ref[pl.ds(dest_ref[j], 1), : row.shape[1]] = row
        return carry

    lax.fori_loop(0, m2l_ref.shape[0], step, 0, unroll=4)


def near_kernel(
    capacity,
    slots_ref,
    recv_ref,
    obs_ref,
    source_matrix_ref,
    target_matrix_ref,
    out_ref,
    source_ref,
    target_ref,
    charge_ref,
    left_a,
    left_b,
    total_a,
    total_b,
):
    rows = 4 * capacity + 8
    blocks = out_ref.shape[0] // GROUP
    side = out_ref.shape[1]
    sub = lax.broadcasted_iota(jnp.int32, (GROUP, side), 0)

    def prepare(i, carry):
        first = pl.multiple_of(i * 2 * GROUP, 2 * GROUP)
        sources, targets = [], []
        for g in range(2):
            slot = pl.multiple_of(first + g * GROUP, GROUP)
            dev = slot // capacity
            column = slot - dev * capacity
            base = dev * rows
            at = pl.multiple_of(base + column, GROUP)
            coords = [recv_ref[pl.ds(at + c * capacity, GROUP), :] - 1.0 for c in range(3)]
            sources.append(piece_rows(coords, 0.0, 1.0))
            charge_ref[pl.ds(slot, GROUP), :] = recv_ref[pl.ds(at + 3 * capacity, GROUP), :]
            tile = recv_ref[pl.ds(pl.multiple_of(base + 4 * capacity, GROUP), GROUP), :]
            centers = pltpu.roll(tile, lax.rem(side - column, side), 1).T
            points = [
                (centers[:GROUP, c : c + 1] - 1.0) + HALF_WIDTH * obs_ref[c, pl.ds(slot, GROUP), :]
                for c in range(3)
            ]
            targets.append(piece_rows(points, SOFT_SQ, -2.0))
        spread(source_matrix_ref, sources, source_ref, first)
        spread(target_matrix_ref, targets, target_ref, first)
        return carry

    lax.fori_loop(0, blocks // 2, prepare, 0, unroll=2)

    def turn(block, u, left_ref):
        left_ref[u] = target_ref[block * GROUP + u].T

    def pair_work(block, u, left_ref, total_ref):
        left = left_ref[u]
        at = (block * GROUP + u) * GROUP
        total = None
        for p in range(4):
            first, second = slots_ref[at + 2 * p], slots_ref[at + 2 * p + 1]
            right = jnp.concatenate([source_ref[first], source_ref[second]], axis=1)
            inverse = lax.rsqrt(jnp.dot(left, right, preferred_element_type=F32))
            part = (
                inverse[:, :128] * charge_ref[pl.ds(first, 1), :]
                + inverse[:, 128:] * charge_ref[pl.ds(second, 1), :]
            )
            total = part if total is None else total + part
        total_ref[u] = total

    def half(before, block, after, left_now, left_next, total_before, total_now):
        sums = None
        for u in range(GROUP):
            turn(after, u, left_next)
            pair_work(block, u, left_now, total_now)
            part = lane_sums(total_before[u])
            sums = part if sums is None else jnp.where(sub == u, part, sums)
        out_ref[pl.ds(pl.multiple_of(before * GROUP, GROUP), GROUP), :] = sums

    for u in range(GROUP):
        turn(0, u, left_a)
    total_b[...] = jnp.zeros_like(total_b)

    def step(i, carry):
        one, two = 2 * i, 2 * i + 1
        half(jnp.maximum(one - 1, 0), one, two, left_a, left_b, total_b, total_a)
        half(one, two, jnp.minimum(two + 1, blocks - 1), left_b, left_a, total_a, total_b)
        return carry

    lax.fori_loop(0, blocks // 2, step, 0)
    sums = None
    for u in range(GROUP):
        part = lane_sums(total_b[u])
        sums = part if sums is None else jnp.where(sub == u, part, sums)
    out_ref[pl.ds((blocks - 1) * GROUP, GROUP), :] = sums


def far_kernel(dens_ref, obs_ref, near_ref, live_ref, out_ref, turned_ref, point_ref, far_ref):
    axis, surface = surface_grid()
    number = {point: q for q, point in enumerate(surface)}
    side = out_ref.shape[1]

    def tile(t, carry):
        first = pl.multiple_of(t * side, side)
        for column in range(0, dens_ref.shape[1], side):
            turned_ref[pl.ds(column, side), :] = dens_ref[pl.ds(first, side), pl.ds(column, side)].T
        for c in range(3):
            point_ref[c] = obs_ref[c, pl.ds(first, side), :].T

        def points(b, carry):
            place = pl.ds(pl.multiple_of(b * GROUP, GROUP), GROUP)
            squares = []
            for c in range(3):
                value = point_ref[c, place, :]
                squares.append([(value - at) * (value - at) for at in axis])
            totals = [jnp.zeros((GROUP, side), F32) for _ in range(4)]
            turn = 0
            for j in range(ORDER):
                for k in range(ORDER):
                    partial = squares[1][j] + squares[2][k]
                    for i in range(ORDER):
                        q = number.get((i, j, k))
                        if q is None:
                            continue
                        inverse = lax.rsqrt(squares[0][i] + partial)
                        totals[turn] = totals[turn] + inverse * turned_ref[pl.ds(q, 1), :]
                        turn = (turn + 1) % 4
            far_ref[place, :] = (totals[0] + totals[1]) + (totals[2] + totals[3])
            return carry

        lax.fori_loop(0, side // GROUP, points, 0)
        near = near_ref[pl.ds(first, side), :].T
        total = far_ref[...] * (1.0 / (FOUR_PI * HALF_WIDTH)) + near * (1.0 / FOUR_PI)
        total = jnp.where(live_ref[pl.ds(t, 1), :] > 0, total, 0.0)
        out_ref[pl.ds(first, side), :] = total.T
        return carry

    lax.fori_loop(0, out_ref.shape[0] // side, tile, 0)


def on_device(
    parent_local,
    parent_slot,
    child_octant,
    child_m2l,
    l2l_ops,
    leaf_center,
    src_coords,
    src_charge,
    obs_owner,
    obs_offset,
    near_slots,
):
    n_dev = lax.axis_size(AXES)
    leaf_dev, width = child_m2l.shape
    slot_table = obs_offset.shape[0]
    points = obs_offset.shape[2]
    capacity = slot_table // n_dev
    block_rows = 4 * capacity + 8
    lanes = -(-width // points) * points
    my_index = lax.axis_index(AXES)
    vmem, smem = pl.BlockSpec(memory_space=pltpu.VMEM), pl.BlockSpec(memory_space=pltpu.SMEM)
    params = pltpu.CompilerParams(vmem_limit_bytes=VMEM_LIMIT)

    mine = lax.dynamic_slice_in_dim(obs_owner, my_index * leaf_dev, leaf_dev)
    leaf_at = jnp.arange(leaf_dev, dtype=jnp.int32)
    same = (mine[:, None] == mine[None, :]) & (leaf_at[None, :] < leaf_at[:, None])
    rank = jnp.sum(same.astype(jnp.int32), axis=1)
    rim_rows = from_behind(parent_local[parent_local.shape[0] - RIM :], AXES, 1)
    packed = pl.pallas_call(
        functools.partial(pack_sources, capacity),
        out_shape=jax.ShapeDtypeStruct((n_dev * block_rows, points), F32),
        in_specs=[smem, smem, smem, vmem, vmem],
        out_specs=vmem,
        compiler_params=params,
        name="pack_sources",
    )(mine, rank, leaf_center.T.reshape(-1), src_coords.transpose(1, 0, 2), src_charge)
    packed, rim_rows, obs_owner, near_slots = lax.optimization_barrier(
        (packed, rim_rows, obs_owner, near_slots)
    )
    counts = jnp.sum((obs_owner.reshape(n_dev, leaf_dev) == my_index).astype(jnp.int32), axis=1)
    live = (jnp.arange(capacity, dtype=jnp.int32)[None, :] < counts[:, None]).astype(jnp.int32).reshape(slot_table)

    live = live.reshape(slot_table // points, points)
    slots = near_slots.reshape(-1)
    recv = lax.all_to_all(
        packed.reshape(n_dev, block_rows, points), AXES, split_axis=0, concat_axis=0, tiled=True
    ).reshape(n_dev * block_rows, points)

    parents = jnp.concatenate([rim_rows, parent_local], axis=0)
    moved = jnp.einsum("pr,oqr->opq", parents, l2l_ops, precision=lax.Precision.HIGHEST)
    stacked = moved.reshape(8 * parents.shape[0], width)
    leaf_local, packed_dens = pl.pallas_call(
        route_leaves,
        out_shape=(
            jax.ShapeDtypeStruct((leaf_dev, width), F32),
            jax.ShapeDtypeStruct((slot_table, lanes), F32),
        ),
        in_specs=[smem, smem, vmem, vmem],
        out_specs=(vmem, vmem),
        compiler_params=params,
        name="route_leaves",
    )(child_octant * parents.shape[0] + parent_slot, mine * capacity + rank, child_m2l, stacked)
    packed_dens, slots, live = lax.optimization_barrier((packed_dens, slots, live))
    dens = lax.all_to_all(
        packed_dens.reshape(n_dev, capacity, lanes), AXES, split_axis=0, concat_axis=0, tiled=True
    ).reshape(slot_table, lanes)

    obs = obs_offset.transpose(1, 0, 2)
    pairs = slot_table * near_slots.shape[1] * points * points
    near = pl.pallas_call(
        functools.partial(near_kernel, capacity),
        out_shape=jax.ShapeDtypeStruct((slot_table, points), F32),
        in_specs=[smem, vmem, vmem, vmem, vmem],
        out_specs=vmem,
        scratch_shapes=[
            pltpu.VMEM((slot_table, FEATS, points), BF16),
            pltpu.VMEM((slot_table, FEATS, points), BF16),
            pltpu.VMEM((slot_table, points), F32),
            pltpu.VMEM((GROUP, points, FEATS), BF16),
            pltpu.VMEM((GROUP, points, FEATS), BF16),
            pltpu.VMEM((GROUP, points, points), F32),
            pltpu.VMEM((GROUP, points, points), F32),
        ],
        compiler_params=params,
        cost_estimate=pl.CostEstimate(flops=70 * pairs, bytes_accessed=5 * 10**6, transcendentals=pairs),
        name="near_field",
    )(
        slots,
        recv,
        obs,
        jnp.asarray(spread_matrix(SOURCE_ORDER, False)),
        jnp.asarray(spread_matrix(TARGET_ORDER, True)),
    )
    potential = pl.pallas_call(
        far_kernel,
        out_shape=jax.ShapeDtypeStruct((slot_table, points), F32),
        in_specs=[vmem, vmem, vmem, vmem],
        out_specs=vmem,
        scratch_shapes=[
            pltpu.VMEM((lanes, points), F32),
            pltpu.VMEM((3, points, points), F32),
            pltpu.VMEM((points, points), F32),
        ],
        compiler_params=params,
        cost_estimate=pl.CostEstimate(flops=10**10, bytes_accessed=5 * 10**6, transcendentals=10**7),
        name="far_field",
    )(dens, obs, near, live)
    return (leaf_local, potential)


def solution(mesh):
    placed = (
        P(AXES, None),
        P(AXES),
        P(AXES),
        P(AXES, None),
        P(),
        P(AXES, None),
        P(AXES, None, None),
        P(AXES, None),
        P(),
        P(AXES, None, None),
        P(AXES, None),
    )
    return jax.shard_map(
        on_device,
        mesh=mesh,
        in_specs=placed,
        out_specs=(P(AXES, None), P(AXES, None)),
        check_vma=False,
    )
```

```python
import functools
import math

import jax
import jax.numpy as jnp
import numpy as np
from jax import lax
from jax.experimental import pallas as pl
from jax.experimental.pallas import tpu as pltpu
from jax.sharding import PartitionSpec as P

ORDER = 8
RIM = 16
RADIUS = 2.95
HALF_WIDTH = 0.5
SOFT_SQ = 0.0025
FOUR_PI = 4.0 * math.pi
AXES = ("grp", "dom")
FEATS = 32
GROUP = 8
VMEM_LIMIT = 40 * 1024 * 1024

F32 = jnp.float32
BF16 = jnp.bfloat16


def from_behind(block, axis, distance):
    devices = range(lax.axis_size(axis))
    route = [(i - distance, i) for i in devices if i - distance in devices]
    return lax.ppermute(block, axis, route)


def surface_grid():
    axis = (np.linspace(-1.0, 1.0, ORDER) * RADIUS).astype(np.float32)
    ends = (0, ORDER - 1)
    points = [
        (i, j, k)
        for i in range(ORDER)
        for j in range(ORDER)
        for k in range(ORDER)
        if i in ends or j in ends or k in ends
    ]
    return [float(value) for value in axis], points


def split(value):
    high = value.astype(BF16)
    rest = value - high.astype(F32)
    mid = rest.astype(BF16)
    return high, mid, (rest - mid.astype(F32)).astype(BF16)


SOURCE_ORDER = ("h", "h", "h", "m", "m", "l")
TARGET_ORDER = ("h", "m", "l", "h", "m", "h")
N_PIECES = 13
PACK = 2 * GROUP


def spread_matrix(order, norm_first):
    start = {"h": 0, "m": 3, "l": 6}
    pieces = [start[name] + c for c in range(3) for name in order]
    pieces += [9, 10, 11, 12, 12, 12] if norm_first else [12, 12, 12, 9, 10, 11]
    table = np.zeros((PACK * FEATS, N_PIECES * PACK), jnp.bfloat16)
    for u in range(PACK):
        for f, piece in enumerate(pieces):
            table[u * FEATS + f, piece * PACK + u] = 1.0
    return table


def piece_rows(coords, extra, scale):
    norm = coords[0] * coords[0] + coords[1] * coords[1] + coords[2] * coords[2] + extra
    parts = [split(scale * value) for value in coords]
    rows = [part[level] for level in range(3) for part in parts]
    rows += list(split(norm)) + [jnp.ones(norm.shape, BF16)]
    return jnp.concatenate(rows, axis=0)


def spread(matrix_ref, blocks, out_ref, slot):
    pieces = jnp.concatenate(blocks, axis=1)
    rows = jnp.dot(matrix_ref[...], pieces, preferred_element_type=F32)
    lanes = blocks[0].shape[1]
    for i in range(2):
        block = rows[:, i * lanes : (i + 1) * lanes].astype(BF16).reshape(PACK, FEATS, lanes)
        out_ref[pl.ds(slot + i * PACK, PACK)] = block


def lane_sums(block):
    high = block.astype(BF16)
    low = (block - high.astype(F32)).astype(BF16)
    ones = jnp.ones((GROUP, 2 * block.shape[1]), BF16)
    pieces = jnp.concatenate([high, low], axis=1)
    return lax.dot_general(ones, pieces, (((1,), (1,)), ((), ())), preferred_element_type=F32)


def pack_sources(capacity, owner_ref, rank_ref, center_ref, coords_ref, charge_ref, out_ref):
    rows = 4 * capacity + 8
    leaves = charge_ref.shape[0]
    lane = lax.broadcasted_iota(jnp.int32, (8, 128), 1)
    sub = lax.broadcasted_iota(jnp.int32, (8, 128), 0)
    out_ref[...] = jnp.zeros_like(out_ref)

    def step(j, carry):
        rank = rank_ref[j]
        base = owner_ref[j] * rows
        for c in range(3):
            out_ref[pl.ds(base + c * capacity + rank, 1), :] = coords_ref[c, pl.ds(j, 1), :]
        out_ref[pl.ds(base + 3 * capacity + rank, 1), :] = charge_ref[pl.ds(j, 1), :]
        place = pl.ds(pl.multiple_of(base + 4 * capacity, 8), 8)
        value = jnp.where(
            sub == 0,
            center_ref[j],
            jnp.where(sub == 1, center_ref[leaves + j], center_ref[2 * leaves + j]),
        )
        out_ref[place, :] = jnp.where(lane == rank, value, out_ref[place, :])
        return carry

    lax.fori_loop(0, leaves, step, 0, unroll=4)


def route_leaves(index_ref, dest_ref, m2l_ref, moved_ref, leaf_ref, out_ref):
    def step(j, carry):
        row = m2l_ref[pl.ds(j, 1), :] + moved_ref[pl.ds(index_ref[j], 1), :]
        leaf_ref[pl.ds(j, 1), :] = row
        out_ref[pl.ds(dest_ref[j], 1), : row.shape[1]] = row
        return carry

    lax.fori_loop(0, m2l_ref.shape[0], step, 0, unroll=4)


def near_kernel(
    capacity,
    slots_ref,
    recv_ref,
    obs_ref,
    source_matrix_ref,
    target_matrix_ref,
    out_ref,
    source_ref,
    target_ref,
    charge_ref,
    left_a,
    left_b,
    total_a,
    total_b,
):
    rows = 4 * capacity + 8
    blocks = out_ref.shape[0] // GROUP
    side = out_ref.shape[1]
    sub = lax.broadcasted_iota(jnp.int32, (GROUP, side), 0)

    def group_points(slot):
        dev = slot // capacity
        column = slot - dev * capacity
        base = dev * rows
        at = pl.multiple_of(base + column, GROUP)
        coords = [recv_ref[pl.ds(at + c * capacity, GROUP), :] - 1.0 for c in range(3)]
        charge_ref[pl.ds(slot, GROUP), :] = recv_ref[pl.ds(at + 3 * capacity, GROUP), :]
        tile = recv_ref[pl.ds(pl.multiple_of(base + 4 * capacity, GROUP), GROUP), :]
        centers = pltpu.roll(tile, lax.rem(side - column, side), 1).T
        targets = [
            (centers[:GROUP, c : c + 1] - 1.0) + HALF_WIDTH * obs_ref[c, pl.ds(slot, GROUP), :]
            for c in range(3)
        ]
        return coords, targets

    def prepare(i, carry):
        first = pl.multiple_of(i * 2 * PACK, 2 * PACK)
        sources, targets = [], []
        for half in range(2):
            one, two = (
                group_points(pl.multiple_of(first + half * PACK + g * GROUP, GROUP)) for g in range(2)
            )
            coords, points = (
                [jnp.concatenate([left, right], axis=0) for left, right in zip(one[k], two[k])]
                for k in range(2)
            )
            sources.append(piece_rows(coords, 0.0, 1.0))
            targets.append(piece_rows(points, SOFT_SQ, -2.0))
        spread(source_matrix_ref, sources, source_ref, first)
        spread(target_matrix_ref, targets, target_ref, first)
        return carry

    lax.fori_loop(0, out_ref.shape[0] // (2 * PACK), prepare, 0, unroll=2)

    def turn(block, u, left_ref):
        left_ref[u] = target_ref[block * GROUP + u].T

    def pair_work(block, u, left_ref, total_ref):
        left = left_ref[u]
        at = (block * GROUP + u) * GROUP
        total = None
        for p in range(4):
            first, second = slots_ref[at + 2 * p], slots_ref[at + 2 * p + 1]
            right = jnp.concatenate([source_ref[first], source_ref[second]], axis=1)
            inverse = lax.rsqrt(jnp.dot(left, right, preferred_element_type=F32))
            part = (
                inverse[:, :128] * charge_ref[pl.ds(first, 1), :]
                + inverse[:, 128:] * charge_ref[pl.ds(second, 1), :]
            )
            total = part if total is None else total + part
        total_ref[u] = total

    def half(before, block, after, left_now, left_next, total_before, total_now):
        sums = None
        for u in range(GROUP):
            turn(after, u, left_next)
            pair_work(block, u, left_now, total_now)
            part = lane_sums(total_before[u])
            sums = part if sums is None else jnp.where(sub == u, part, sums)
        out_ref[pl.ds(pl.multiple_of(before * GROUP, GROUP), GROUP), :] = sums

    for u in range(GROUP):
        turn(0, u, left_a)
    total_b[...] = jnp.zeros_like(total_b)

    def step(i, carry):
        one, two = 2 * i, 2 * i + 1
        half(jnp.maximum(one - 1, 0), one, two, left_a, left_b, total_b, total_a)
        half(one, two, jnp.minimum(two + 1, blocks - 1), left_b, left_a, total_a, total_b)
        return carry

    lax.fori_loop(0, blocks // 2, step, 0)
    sums = None
    for u in range(GROUP):
        part = lane_sums(total_b[u])
        sums = part if sums is None else jnp.where(sub == u, part, sums)
    out_ref[pl.ds((blocks - 1) * GROUP, GROUP), :] = sums


def far_kernel(dens_ref, obs_ref, near_ref, live_ref, out_ref, turned_ref, point_ref, far_ref):
    axis, surface = surface_grid()
    number = {point: q for q, point in enumerate(surface)}
    side = out_ref.shape[1]

    def tile(t, carry):
        first = pl.multiple_of(t * side, side)
        for column in range(0, dens_ref.shape[1], side):
            turned_ref[pl.ds(column, side), :] = dens_ref[pl.ds(first, side), pl.ds(column, side)].T
        for c in range(3):
            point_ref[c] = obs_ref[c, pl.ds(first, side), :].T

        def points(b, carry):
            place = pl.ds(pl.multiple_of(b * GROUP, GROUP), GROUP)
            squares = []
            for c in range(3):
                value = point_ref[c, place, :]
                squares.append([(value - at) * (value - at) for at in axis])
            totals = [jnp.zeros((GROUP, side), F32) for _ in range(4)]
            turn = 0
            for j in range(ORDER):
                for k in range(ORDER):
                    partial = squares[1][j] + squares[2][k]
                    for i in range(ORDER):
                        q = number.get((i, j, k))
                        if q is None:
                            continue
                        inverse = lax.rsqrt(squares[0][i] + partial)
                        totals[turn] = totals[turn] + inverse * turned_ref[pl.ds(q, 1), :]
                        turn = (turn + 1) % 4
            far_ref[place, :] = (totals[0] + totals[1]) + (totals[2] + totals[3])
            return carry

        lax.fori_loop(0, side // GROUP, points, 0, unroll=2)
        near = near_ref[pl.ds(first, side), :].T
        total = far_ref[...] * (1.0 / (FOUR_PI * HALF_WIDTH)) + near * (1.0 / FOUR_PI)
        total = jnp.where(live_ref[pl.ds(t, 1), :] > 0, total, 0.0)
        out_ref[pl.ds(first, side), :] = total.T
        return carry

    lax.fori_loop(0, out_ref.shape[0] // side, tile, 0)


def on_device(
    parent_local,
    parent_slot,
    child_octant,
    child_m2l,
    l2l_ops,
    leaf_center,
    src_coords,
    src_charge,
    obs_owner,
    obs_offset,
    near_slots,
):
    n_dev = lax.axis_size(AXES)
    leaf_dev, width = child_m2l.shape
    slot_table = obs_offset.shape[0]
    points = obs_offset.shape[2]
    capacity = slot_table // n_dev
    block_rows = 4 * capacity + 8
    lanes = -(-width // points) * points
    my_index = lax.axis_index(AXES)
    vmem, smem = pl.BlockSpec(memory_space=pltpu.VMEM), pl.BlockSpec(memory_space=pltpu.SMEM)
    params = pltpu.CompilerParams(vmem_limit_bytes=VMEM_LIMIT)

    mine = lax.dynamic_slice_in_dim(obs_owner, my_index * leaf_dev, leaf_dev)
    leaf_at = jnp.arange(leaf_dev, dtype=jnp.int32)
    same = (mine[:, None] == mine[None, :]) & (leaf_at[None, :] < leaf_at[:, None])
    rank = jnp.sum(same.astype(jnp.int32), axis=1)
    rim_rows = from_behind(parent_local[parent_local.shape[0] - RIM :], AXES, 1)
    packed = pl.pallas_call(
        functools.partial(pack_sources, capacity),
        out_shape=jax.ShapeDtypeStruct((n_dev * block_rows, points), F32),
        in_specs=[smem, smem, smem, vmem, vmem],
        out_specs=vmem,
        compiler_params=params,
        name="pack_sources",
    )(mine, rank, leaf_center.T.reshape(-1), src_coords.transpose(1, 0, 2), src_charge)
    packed, rim_rows, obs_owner, near_slots = lax.optimization_barrier(
        (packed, rim_rows, obs_owner, near_slots)
    )
    counts = jnp.sum((obs_owner.reshape(n_dev, leaf_dev) == my_index).astype(jnp.int32), axis=1)
    live = (jnp.arange(capacity, dtype=jnp.int32)[None, :] < counts[:, None]).astype(jnp.int32).reshape(slot_table)

    live = live.reshape(slot_table // points, points)
    slots = near_slots.reshape(-1)
    recv = lax.all_to_all(
        packed.reshape(n_dev, block_rows, points), AXES, split_axis=0, concat_axis=0, tiled=True
    ).reshape(n_dev * block_rows, points)

    parents = jnp.concatenate([rim_rows, parent_local], axis=0)
    moved = jnp.einsum("pr,oqr->opq", parents, l2l_ops, precision=lax.Precision.HIGHEST)
    stacked = moved.reshape(8 * parents.shape[0], width)
    leaf_local, packed_dens = pl.pallas_call(
        route_leaves,
        out_shape=(
            jax.ShapeDtypeStruct((leaf_dev, width), F32),
            jax.ShapeDtypeStruct((slot_table, lanes), F32),
        ),
        in_specs=[smem, smem, vmem, vmem],
        out_specs=(vmem, vmem),
        compiler_params=params,
        name="route_leaves",
    )(child_octant * parents.shape[0] + parent_slot, mine * capacity + rank, child_m2l, stacked)
    packed_dens, slots, live = lax.optimization_barrier((packed_dens, slots, live))
    dens = lax.all_to_all(
        packed_dens.reshape(n_dev, capacity, lanes), AXES, split_axis=0, concat_axis=0, tiled=True
    ).reshape(slot_table, lanes)

    obs = obs_offset.transpose(1, 0, 2)
    pairs = slot_table * near_slots.shape[1] * points * points
    near = pl.pallas_call(
        functools.partial(near_kernel, capacity),
        out_shape=jax.ShapeDtypeStruct((slot_table, points), F32),
        in_specs=[smem, vmem, vmem, vmem, vmem],
        out_specs=vmem,
        scratch_shapes=[
            pltpu.VMEM((slot_table, FEATS, points), BF16),
            pltpu.VMEM((slot_table, FEATS, points), BF16),
            pltpu.VMEM((slot_table, points), F32),
            pltpu.VMEM((GROUP, points, FEATS), BF16),
            pltpu.VMEM((GROUP, points, FEATS), BF16),
            pltpu.VMEM((GROUP, points, points), F32),
            pltpu.VMEM((GROUP, points, points), F32),
        ],
        compiler_params=params,
        cost_estimate=pl.CostEstimate(flops=70 * pairs, bytes_accessed=5 * 10**6, transcendentals=pairs),
        name="near_field",
    )(
        slots,
        recv,
        obs,
        jnp.asarray(spread_matrix(SOURCE_ORDER, False)),
        jnp.asarray(spread_matrix(TARGET_ORDER, True)),
    )
    potential = pl.pallas_call(
        far_kernel,
        out_shape=jax.ShapeDtypeStruct((slot_table, points), F32),
        in_specs=[vmem, vmem, vmem, vmem],
        out_specs=vmem,
        scratch_shapes=[
            pltpu.VMEM((lanes, points), F32),
            pltpu.VMEM((3, points, points), F32),
            pltpu.VMEM((points, points), F32),
        ],
        compiler_params=params,
        cost_estimate=pl.CostEstimate(flops=10**10, bytes_accessed=5 * 10**6, transcendentals=10**7),
        name="far_field",
    )(dens, obs, near, live)
    return (leaf_local, potential)


def solution(mesh):
    placed = (
        P(AXES, None),
        P(AXES),
        P(AXES),
        P(AXES, None),
        P(),
        P(AXES, None),
        P(AXES, None, None),
        P(AXES, None),
        P(),
        P(AXES, None, None),
        P(AXES, None),
    )
    return jax.shard_map(
        on_device,
        mesh=mesh,
        in_specs=placed,
        out_specs=(P(AXES, None), P(AXES, None)),
        check_vma=False,
    )
```

```python
import functools
import math

import jax
import jax.numpy as jnp
import numpy as np
from jax import lax
from jax.experimental import pallas as pl
from jax.experimental.pallas import tpu as pltpu
from jax.sharding import PartitionSpec as P

ORDER = 8
RIM = 16
RADIUS = 2.95
HALF_WIDTH = 0.5
SOFT_SQ = 0.0025
FOUR_PI = 4.0 * math.pi
AXES = ("grp", "dom")
FEATS = 32
GROUP = 8
VMEM_LIMIT = 40 * 1024 * 1024

F32 = jnp.float32
BF16 = jnp.bfloat16


def from_behind(block, axis, distance):
    devices = range(lax.axis_size(axis))
    route = [(i - distance, i) for i in devices if i - distance in devices]
    return lax.ppermute(block, axis, route)


def surface_grid():
    axis = (np.linspace(-1.0, 1.0, ORDER) * RADIUS).astype(np.float32)
    ends = (0, ORDER - 1)
    points = [
        (i, j, k)
        for i in range(ORDER)
        for j in range(ORDER)
        for k in range(ORDER)
        if i in ends or j in ends or k in ends
    ]
    return [float(value) for value in axis], points


def split(value):
    high = value.astype(BF16)
    rest = value - high.astype(F32)
    mid = rest.astype(BF16)
    return high, mid, (rest - mid.astype(F32)).astype(BF16)


SOURCE_ORDER = ("h", "h", "h", "m", "m", "l")
TARGET_ORDER = ("h", "m", "l", "h", "m", "h")
N_PIECES = 13
PACK = 2 * GROUP


def spread_matrix(order, norm_first):
    start = {"h": 0, "m": 3, "l": 6}
    pieces = [start[name] + c for c in range(3) for name in order]
    pieces += [9, 10, 11, 12, 12, 12] if norm_first else [12, 12, 12, 9, 10, 11]
    table = np.zeros((PACK * FEATS, N_PIECES * PACK), jnp.bfloat16)
    for u in range(PACK):
        for f, piece in enumerate(pieces):
            table[u * FEATS + f, piece * PACK + u] = 1.0
    return table


def piece_rows(coords, extra, scale):
    norm = coords[0] * coords[0] + coords[1] * coords[1] + coords[2] * coords[2] + extra
    parts = [split(scale * value) for value in coords]
    rows = [part[level] for level in range(3) for part in parts]
    rows += list(split(norm)) + [jnp.ones(norm.shape, BF16)]
    return jnp.concatenate(rows, axis=0)


def spread(matrix_ref, blocks, out_ref, slot):
    pieces = jnp.concatenate(blocks, axis=1)
    rows = jnp.dot(matrix_ref[...], pieces, preferred_element_type=F32)
    lanes = blocks[0].shape[1]
    for i in range(2):
        block = rows[:, i * lanes : (i + 1) * lanes].astype(BF16).reshape(PACK, FEATS, lanes)
        out_ref[pl.ds(slot + i * PACK, PACK)] = block


def lane_sums(block):
    high = block.astype(BF16)
    low = (block - high.astype(F32)).astype(BF16)
    ones = jnp.ones((GROUP, 2 * block.shape[1]), BF16)
    pieces = jnp.concatenate([high, low], axis=1)
    return lax.dot_general(ones, pieces, (((1,), (1,)), ((), ())), preferred_element_type=F32)


def pack_sources(capacity, owner_ref, rank_ref, center_ref, coords_ref, charge_ref, out_ref):
    rows = 4 * capacity + 8
    leaves = charge_ref.shape[0]
    lane = lax.broadcasted_iota(jnp.int32, (8, 128), 1)
    sub = lax.broadcasted_iota(jnp.int32, (8, 128), 0)
    out_ref[...] = jnp.zeros_like(out_ref)

    def step(j, carry):
        rank = rank_ref[j]
        base = owner_ref[j] * rows
        for c in range(3):
            out_ref[pl.ds(base + c * capacity + rank, 1), :] = coords_ref[c, pl.ds(j, 1), :]
        out_ref[pl.ds(base + 3 * capacity + rank, 1), :] = charge_ref[pl.ds(j, 1), :]
        place = pl.ds(pl.multiple_of(base + 4 * capacity, 8), 8)
        value = jnp.where(
            sub == 0,
            center_ref[j],
            jnp.where(sub == 1, center_ref[leaves + j], center_ref[2 * leaves + j]),
        )
        pltpu.store(out_ref.at[place, :], value, mask=lane == rank)
        return carry

    lax.fori_loop(0, leaves, step, 0, unroll=8)


def route_leaves(index_ref, dest_ref, m2l_ref, moved_ref, leaf_ref, out_ref):
    def step(j, carry):
        row = m2l_ref[pl.ds(j, 1), :] + moved_ref[pl.ds(index_ref[j], 1), :]
        leaf_ref[pl.ds(j, 1), :] = row
        out_ref[pl.ds(dest_ref[j], 1), : row.shape[1]] = row
        return carry

    lax.fori_loop(0, m2l_ref.shape[0], step, 0, unroll=4)


def near_kernel(
    capacity,
    slots_ref,
    recv_ref,
    obs_ref,
    source_matrix_ref,
    target_matrix_ref,
    out_ref,
    source_ref,
    target_ref,
    charge_ref,
    left_a,
    left_b,
    total_a,
    total_b,
):
    rows = 4 * capacity + 8
    blocks = out_ref.shape[0] // GROUP
    side = out_ref.shape[1]
    sub = lax.broadcasted_iota(jnp.int32, (GROUP, side), 0)

    def group_points(slot):
        dev = slot // capacity
        column = slot - dev * capacity
        base = dev * rows
        at = pl.multiple_of(base + column, GROUP)
        coords = [recv_ref[pl.ds(at + c * capacity, GROUP), :] - 1.0 for c in range(3)]
        charge_ref[pl.ds(slot, GROUP), :] = recv_ref[pl.ds(at + 3 * capacity, GROUP), :]
        tile = recv_ref[pl.ds(pl.multiple_of(base + 4 * capacity, GROUP), GROUP), :]
        centers = pltpu.roll(tile, lax.rem(side - column, side), 1).T
        targets = [
            (centers[:GROUP, c : c + 1] - 1.0) + HALF_WIDTH * obs_ref[c, pl.ds(slot, GROUP), :]
            for c in range(3)
        ]
        return coords, targets

    def prepare(i, carry):
        first = pl.multiple_of(i * 2 * PACK, 2 * PACK)
        sources, targets = [], []
        for half in range(2):
            one, two = (
                group_points(pl.multiple_of(first + half * PACK + g * GROUP, GROUP)) for g in range(2)
            )
            coords, points = (
                [jnp.concatenate([left, right], axis=0) for left, right in zip(one[k], two[k])]
                for k in range(2)
            )
            sources.append(piece_rows(coords, 0.0, 1.0))
            targets.append(piece_rows(points, SOFT_SQ, -2.0))
        spread(source_matrix_ref, sources, source_ref, first)
        spread(target_matrix_ref, targets, target_ref, first)
        return carry

    lax.fori_loop(0, out_ref.shape[0] // (2 * PACK), prepare, 0, unroll=4)

    def turn(block, u, left_ref):
        left_ref[u] = target_ref[block * GROUP + u].T

    def pair_work(block, u, left_ref, total_ref):
        left = left_ref[u]
        at = (block * GROUP + u) * GROUP
        total = None
        for p in range(4):
            first, second = slots_ref[at + 2 * p], slots_ref[at + 2 * p + 1]
            right = jnp.concatenate([source_ref[first], source_ref[second]], axis=1)
            inverse = lax.rsqrt(jnp.dot(left, right, preferred_element_type=F32))
            part = (
                inverse[:, :128] * charge_ref[pl.ds(first, 1), :]
                + inverse[:, 128:] * charge_ref[pl.ds(second, 1), :]
            )
            total = part if total is None else total + part
        total_ref[u] = total

    def half(before, block, after, left_now, left_next, total_before, total_now):
        sums = None
        for u in range(GROUP):
            turn(after, u, left_next)
            pair_work(block, u, left_now, total_now)
            part = lane_sums(total_before[u])
            sums = part if sums is None else jnp.where(sub == u, part, sums)
        out_ref[pl.ds(pl.multiple_of(before * GROUP, GROUP), GROUP), :] = sums

    for u in range(GROUP):
        turn(0, u, left_a)
    total_b[...] = jnp.zeros_like(total_b)

    def step(i, carry):
        one, two = 2 * i, 2 * i + 1
        half(jnp.maximum(one - 1, 0), one, two, left_a, left_b, total_b, total_a)
        half(one, two, jnp.minimum(two + 1, blocks - 1), left_b, left_a, total_a, total_b)
        return carry

    lax.fori_loop(0, blocks // 2, step, 0, unroll=2)
    sums = None
    for u in range(GROUP):
        part = lane_sums(total_b[u])
        sums = part if sums is None else jnp.where(sub == u, part, sums)
    out_ref[pl.ds((blocks - 1) * GROUP, GROUP), :] = sums


def far_kernel(dens_ref, obs_ref, near_ref, live_ref, out_ref, turned_ref, point_ref, far_ref):
    axis, surface = surface_grid()
    number = {point: q for q, point in enumerate(surface)}
    side = out_ref.shape[1]

    def tile(t, carry):
        first = pl.multiple_of(t * side, side)
        for column in range(0, dens_ref.shape[1], side):
            turned_ref[pl.ds(column, side), :] = dens_ref[pl.ds(first, side), pl.ds(column, side)].T
        for c in range(3):
            point_ref[c] = obs_ref[c, pl.ds(first, side), :].T

        def points(b, carry):
            place = pl.ds(pl.multiple_of(b * GROUP, GROUP), GROUP)
            squares = []
            for c in range(3):
                value = point_ref[c, place, :]
                squares.append([(value - at) * (value - at) for at in axis])
            totals = [jnp.zeros((GROUP, side), F32) for _ in range(4)]
            turn = 0
            for j in range(ORDER):
                for k in range(ORDER):
                    partial = squares[1][j] + squares[2][k]
                    for i in range(ORDER):
                        q = number.get((i, j, k))
                        if q is None:
                            continue
                        inverse = lax.rsqrt(squares[0][i] + partial)
                        totals[turn] = totals[turn] + inverse * turned_ref[pl.ds(q, 1), :]
                        turn = (turn + 1) % 4
            far_ref[place, :] = (totals[0] + totals[1]) + (totals[2] + totals[3])
            return carry

        lax.fori_loop(0, side // GROUP, points, 0, unroll=2)
        near = near_ref[pl.ds(first, side), :].T
        total = far_ref[...] * (1.0 / (FOUR_PI * HALF_WIDTH)) + near * (1.0 / FOUR_PI)
        total = jnp.where(live_ref[pl.ds(t, 1), :] > 0, total, 0.0)
        out_ref[pl.ds(first, side), :] = total.T
        return carry

    lax.fori_loop(0, out_ref.shape[0] // side, tile, 0)


def on_device(
    parent_local,
    parent_slot,
    child_octant,
    child_m2l,
    l2l_ops,
    leaf_center,
    src_coords,
    src_charge,
    obs_owner,
    obs_offset,
    near_slots,
):
    n_dev = lax.axis_size(AXES)
    leaf_dev, width = child_m2l.shape
    slot_table = obs_offset.shape[0]
    points = obs_offset.shape[2]
    capacity = slot_table // n_dev
    block_rows = 4 * capacity + 8
    lanes = -(-width // points) * points
    my_index = lax.axis_index(AXES)
    vmem, smem = pl.BlockSpec(memory_space=pltpu.VMEM), pl.BlockSpec(memory_space=pltpu.SMEM)
    params = pltpu.CompilerParams(vmem_limit_bytes=VMEM_LIMIT)

    mine = lax.dynamic_slice_in_dim(obs_owner, my_index * leaf_dev, leaf_dev)
    leaf_at = jnp.arange(leaf_dev, dtype=jnp.int32)
    same = (mine[:, None] == mine[None, :]) & (leaf_at[None, :] < leaf_at[:, None])
    rank = jnp.sum(same.astype(jnp.int32), axis=1)
    rim_rows = from_behind(parent_local[parent_local.shape[0] - RIM :], AXES, 1)
    packed = pl.pallas_call(
        functools.partial(pack_sources, capacity),
        out_shape=jax.ShapeDtypeStruct((n_dev * block_rows, points), F32),
        in_specs=[smem, smem, smem, vmem, vmem],
        out_specs=vmem,
        compiler_params=params,
        name="pack_sources",
    )(mine, rank, leaf_center.T.reshape(-1), src_coords.transpose(1, 0, 2), src_charge)
    packed, rim_rows, obs_owner, near_slots = lax.optimization_barrier(
        (packed, rim_rows, obs_owner, near_slots)
    )
    counts = jnp.sum((obs_owner.reshape(n_dev, leaf_dev) == my_index).astype(jnp.int32), axis=1)
    live = (jnp.arange(capacity, dtype=jnp.int32)[None, :] < counts[:, None]).astype(jnp.int32).reshape(slot_table)

    live = live.reshape(slot_table // points, points)
    slots = near_slots.reshape(-1)
    recv = lax.all_to_all(
        packed.reshape(n_dev, block_rows, points), AXES, split_axis=0, concat_axis=0, tiled=True
    ).reshape(n_dev * block_rows, points)

    parents = jnp.concatenate([rim_rows, parent_local], axis=0)
    moved = jnp.einsum("pr,oqr->opq", parents, l2l_ops, precision=lax.Precision.HIGHEST)
    stacked = moved.reshape(8 * parents.shape[0], width)
    leaf_local, packed_dens = pl.pallas_call(
        route_leaves,
        out_shape=(
            jax.ShapeDtypeStruct((leaf_dev, width), F32),
            jax.ShapeDtypeStruct((slot_table, lanes), F32),
        ),
        in_specs=[smem, smem, vmem, vmem],
        out_specs=(vmem, vmem),
        compiler_params=params,
        name="route_leaves",
    )(child_octant * parents.shape[0] + parent_slot, mine * capacity + rank, child_m2l, stacked)
    packed_dens, slots, live = lax.optimization_barrier((packed_dens, slots, live))
    dens = lax.all_to_all(
        packed_dens.reshape(n_dev, capacity, lanes), AXES, split_axis=0, concat_axis=0, tiled=True
    ).reshape(slot_table, lanes)

    obs = obs_offset.transpose(1, 0, 2)
    pairs = slot_table * near_slots.shape[1] * points * points
    near = pl.pallas_call(
        functools.partial(near_kernel, capacity),
        out_shape=jax.ShapeDtypeStruct((slot_table, points), F32),
        in_specs=[smem, vmem, vmem, vmem, vmem],
        out_specs=vmem,
        scratch_shapes=[
            pltpu.VMEM((slot_table, FEATS, points), BF16),
            pltpu.VMEM((slot_table, FEATS, points), BF16),
            pltpu.VMEM((slot_table, points), F32),
            pltpu.VMEM((GROUP, points, FEATS), BF16),
            pltpu.VMEM((GROUP, points, FEATS), BF16),
            pltpu.VMEM((GROUP, points, points), F32),
            pltpu.VMEM((GROUP, points, points), F32),
        ],
        compiler_params=params,
        cost_estimate=pl.CostEstimate(flops=70 * pairs, bytes_accessed=5 * 10**6, transcendentals=pairs),
        name="near_field",
    )(
        slots,
        recv,
        obs,
        jnp.asarray(spread_matrix(SOURCE_ORDER, False)),
        jnp.asarray(spread_matrix(TARGET_ORDER, True)),
    )
    potential = pl.pallas_call(
        far_kernel,
        out_shape=jax.ShapeDtypeStruct((slot_table, points), F32),
        in_specs=[vmem, vmem, vmem, vmem],
        out_specs=vmem,
        scratch_shapes=[
            pltpu.VMEM((lanes, points), F32),
            pltpu.VMEM((3, points, points), F32),
            pltpu.VMEM((points, points), F32),
        ],
        compiler_params=params,
        cost_estimate=pl.CostEstimate(flops=10**10, bytes_accessed=5 * 10**6, transcendentals=10**7),
        name="far_field",
    )(dens, obs, near, live)
    return (leaf_local, potential)


def solution(mesh):
    placed = (
        P(AXES, None),
        P(AXES),
        P(AXES),
        P(AXES, None),
        P(),
        P(AXES, None),
        P(AXES, None, None),
        P(AXES, None),
        P(),
        P(AXES, None, None),
        P(AXES, None),
    )
    return jax.shard_map(
        on_device,
        mesh=mesh,
        in_specs=placed,
        out_specs=(P(AXES, None), P(AXES, None)),
        check_vma=False,
    )
```

```python
import functools
import math

import jax
import jax.numpy as jnp
import numpy as np
from jax import lax
from jax.experimental import pallas as pl
from jax.experimental.pallas import tpu as pltpu
from jax.sharding import PartitionSpec as P

ORDER = 8
RIM = 16
RADIUS = 2.95
HALF_WIDTH = 0.5
SOFT_SQ = 0.0025
FOUR_PI = 4.0 * math.pi
AXES = ("grp", "dom")
FEATS = 32
GROUP = 8
VMEM_LIMIT = 40 * 1024 * 1024

F32 = jnp.float32
BF16 = jnp.bfloat16


def from_behind(block, axis, distance):
    devices = range(lax.axis_size(axis))
    route = [(i - distance, i) for i in devices if i - distance in devices]
    return lax.ppermute(block, axis, route)


def surface_grid():
    axis = (np.linspace(-1.0, 1.0, ORDER) * RADIUS).astype(np.float32)
    ends = (0, ORDER - 1)
    points = [
        (i, j, k)
        for i in range(ORDER)
        for j in range(ORDER)
        for k in range(ORDER)
        if i in ends or j in ends or k in ends
    ]
    return [float(value) for value in axis], points


def split(value):
    high = value.astype(BF16)
    rest = value - high.astype(F32)
    mid = rest.astype(BF16)
    return high, mid, (rest - mid.astype(F32)).astype(BF16)


SOURCE_ORDER = ("h", "h", "h", "m", "m", "l")
TARGET_ORDER = ("h", "m", "l", "h", "m", "h")
N_PIECES = 13
PACK = 2 * GROUP


def spread_matrix(order, norm_first):
    start = {"h": 0, "m": 3, "l": 6}
    pieces = [start[name] + c for c in range(3) for name in order]
    pieces += [9, 10, 11, 12, 12, 12] if norm_first else [12, 12, 12, 9, 10, 11]
    table = np.zeros((PACK * FEATS, N_PIECES * PACK), jnp.bfloat16)
    for u in range(PACK):
        for f, piece in enumerate(pieces):
            table[u * FEATS + f, piece * PACK + u] = 1.0
    return table


def piece_rows(coords, extra, scale):
    norm = coords[0] * coords[0] + coords[1] * coords[1] + coords[2] * coords[2] + extra
    parts = [split(scale * value) for value in coords]
    rows = [part[level] for level in range(3) for part in parts]
    rows += list(split(norm)) + [jnp.ones(norm.shape, BF16)]
    return jnp.concatenate(rows, axis=0)


def spread(matrix_ref, blocks, out_ref, slot):
    pieces = jnp.concatenate(blocks, axis=1)
    rows = jnp.dot(matrix_ref[...], pieces, preferred_element_type=F32)
    lanes = blocks[0].shape[1]
    for i in range(2):
        block = rows[:, i * lanes : (i + 1) * lanes].astype(BF16).reshape(PACK, FEATS, lanes)
        out_ref[pl.ds(slot + i * PACK, PACK)] = block


def lane_sums(block):
    high = block.astype(BF16)
    low = (block - high.astype(F32)).astype(BF16)
    ones = jnp.ones((GROUP, 2 * block.shape[1]), BF16)
    pieces = jnp.concatenate([high, low], axis=1)
    return lax.dot_general(ones, pieces, (((1,), (1,)), ((), ())), preferred_element_type=F32)


def pack_sources(capacity, owner_ref, rank_ref, center_ref, coords_ref, charge_ref, out_ref):
    rows = 4 * capacity + 8
    leaves = charge_ref.shape[0]
    lane = lax.broadcasted_iota(jnp.int32, (8, 128), 1)
    sub = lax.broadcasted_iota(jnp.int32, (8, 128), 0)
    out_ref[...] = jnp.zeros_like(out_ref)

    def step(j, carry):
        rank = rank_ref[j]
        base = owner_ref[j] * rows
        for c in range(3):
            out_ref[pl.ds(base + c * capacity + rank, 1), :] = coords_ref[c, pl.ds(j, 1), :]
        out_ref[pl.ds(base + 3 * capacity + rank, 1), :] = charge_ref[pl.ds(j, 1), :]
        place = pl.ds(pl.multiple_of(base + 4 * capacity, 8), 8)
        value = jnp.where(
            sub == 0,
            center_ref[j],
            jnp.where(sub == 1, center_ref[leaves + j], center_ref[2 * leaves + j]),
        )
        pltpu.store(out_ref.at[place, :], value, mask=lane == rank)
        return carry

    lax.fori_loop(0, leaves, step, 0, unroll=8)


def route_leaves(index_ref, dest_ref, m2l_ref, moved_ref, leaf_ref, out_ref):
    def step(j, carry):
        row = m2l_ref[pl.ds(j, 1), :] + moved_ref[pl.ds(index_ref[j], 1), :]
        leaf_ref[pl.ds(j, 1), :] = row
        out_ref[pl.ds(dest_ref[j], 1), : row.shape[1]] = row
        return carry

    lax.fori_loop(0, m2l_ref.shape[0], step, 0, unroll=4)


def near_kernel(
    capacity,
    slots_ref,
    recv_ref,
    obs_ref,
    source_matrix_ref,
    target_matrix_ref,
    out_ref,
    source_ref,
    target_ref,
    charge_ref,
    left_a,
    left_b,
    total_a,
    total_b,
):
    rows = 4 * capacity + 8
    blocks = out_ref.shape[0] // GROUP
    side = out_ref.shape[1]
    sub = lax.broadcasted_iota(jnp.int32, (GROUP, side), 0)

    def group_points(slot):
        dev = slot // capacity
        column = slot - dev * capacity
        base = dev * rows
        at = pl.multiple_of(base + column, GROUP)
        coords = [recv_ref[pl.ds(at + c * capacity, GROUP), :] - 1.0 for c in range(3)]
        charge_ref[pl.ds(slot, GROUP), :] = recv_ref[pl.ds(at + 3 * capacity, GROUP), :]
        tile = recv_ref[pl.ds(pl.multiple_of(base + 4 * capacity, GROUP), GROUP), :]
        centers = pltpu.roll(tile, lax.rem(side - column, side), 1).T
        targets = [
            (centers[:GROUP, c : c + 1] - 1.0) + HALF_WIDTH * obs_ref[c, pl.ds(slot, GROUP), :]
            for c in range(3)
        ]
        return coords, targets

    def prepare(i, carry):
        first = pl.multiple_of(i * 2 * PACK, 2 * PACK)
        sources, targets = [], []
        for half in range(2):
            one, two = (
                group_points(pl.multiple_of(first + half * PACK + g * GROUP, GROUP)) for g in range(2)
            )
            coords, points = (
                [jnp.concatenate([left, right], axis=0) for left, right in zip(one[k], two[k])]
                for k in range(2)
            )
            sources.append(piece_rows(coords, 0.0, 1.0))
            targets.append(piece_rows(points, SOFT_SQ, -2.0))
        spread(source_matrix_ref, sources, source_ref, first)
        spread(target_matrix_ref, targets, target_ref, first)
        return carry

    lax.fori_loop(0, out_ref.shape[0] // (2 * PACK), prepare, 0, unroll=8)

    def turn(block, u, left_ref):
        left_ref[u] = target_ref[block * GROUP + u].T

    def pair_work(block, u, left_ref, total_ref):
        left = left_ref[u]
        at = (block * GROUP + u) * GROUP
        total = None
        for p in range(4):
            first, second = slots_ref[at + 2 * p], slots_ref[at + 2 * p + 1]
            right = jnp.concatenate([source_ref[first], source_ref[second]], axis=1)
            inverse = lax.rsqrt(jnp.dot(left, right, preferred_element_type=F32))
            part = (
                inverse[:, :128] * charge_ref[pl.ds(first, 1), :]
                + inverse[:, 128:] * charge_ref[pl.ds(second, 1), :]
            )
            total = part if total is None else total + part
        total_ref[u] = total

    def half(before, block, after, left_now, left_next, total_before, total_now):
        sums = None
        for u in range(GROUP):
            turn(after, u, left_next)
            pair_work(block, u, left_now, total_now)
            part = lane_sums(total_before[u])
            sums = part if sums is None else jnp.where(sub == u, part, sums)
        out_ref[pl.ds(pl.multiple_of(before * GROUP, GROUP), GROUP), :] = sums

    for u in range(GROUP):
        turn(0, u, left_a)
    total_b[...] = jnp.zeros_like(total_b)

    def step(i, carry):
        one, two = 2 * i, 2 * i + 1
        half(jnp.maximum(one - 1, 0), one, two, left_a, left_b, total_b, total_a)
        half(one, two, jnp.minimum(two + 1, blocks - 1), left_b, left_a, total_a, total_b)
        return carry

    lax.fori_loop(0, blocks // 2, step, 0, unroll=4)
    sums = None
    for u in range(GROUP):
        part = lane_sums(total_b[u])
        sums = part if sums is None else jnp.where(sub == u, part, sums)
    out_ref[pl.ds((blocks - 1) * GROUP, GROUP), :] = sums


def far_kernel(dens_ref, obs_ref, near_ref, live_ref, out_ref, turned_ref, point_ref, far_ref):
    axis, surface = surface_grid()
    number = {point: q for q, point in enumerate(surface)}
    side = out_ref.shape[1]

    def tile(t, carry):
        first = pl.multiple_of(t * side, side)
        for column in range(0, dens_ref.shape[1], side):
            turned_ref[pl.ds(column, side), :] = dens_ref[pl.ds(first, side), pl.ds(column, side)].T
        for c in range(3):
            point_ref[c] = obs_ref[c, pl.ds(first, side), :].T

        def points(b, carry):
            place = pl.ds(pl.multiple_of(b * GROUP, GROUP), GROUP)
            squares = []
            for c in range(3):
                value = point_ref[c, place, :]
                squares.append([(value - at) * (value - at) for at in axis])
            totals = [jnp.zeros((GROUP, side), F32) for _ in range(4)]
            turn = 0
            for j in range(ORDER):
                for k in range(ORDER):
                    partial = squares[1][j] + squares[2][k]
                    for i in range(ORDER):
                        q = number.get((i, j, k))
                        if q is None:
                            continue
                        inverse = lax.rsqrt(squares[0][i] + partial)
                        totals[turn] = totals[turn] + inverse * turned_ref[pl.ds(q, 1), :]
                        turn = (turn + 1) % 4
            far_ref[place, :] = (totals[0] + totals[1]) + (totals[2] + totals[3])
            return carry

        lax.fori_loop(0, side // GROUP, points, 0, unroll=2)
        near = near_ref[pl.ds(first, side), :].T
        total = far_ref[...] * (1.0 / (FOUR_PI * HALF_WIDTH)) + near * (1.0 / FOUR_PI)
        total = jnp.where(live_ref[pl.ds(t, 1), :] > 0, total, 0.0)
        out_ref[pl.ds(first, side), :] = total.T
        return carry

    lax.fori_loop(0, out_ref.shape[0] // side, tile, 0)


def on_device(
    parent_local,
    parent_slot,
    child_octant,
    child_m2l,
    l2l_ops,
    leaf_center,
    src_coords,
    src_charge,
    obs_owner,
    obs_offset,
    near_slots,
):
    n_dev = lax.axis_size(AXES)
    leaf_dev, width = child_m2l.shape
    slot_table = obs_offset.shape[0]
    points = obs_offset.shape[2]
    capacity = slot_table // n_dev
    block_rows = 4 * capacity + 8
    lanes = -(-width // points) * points
    my_index = lax.axis_index(AXES)
    vmem, smem = pl.BlockSpec(memory_space=pltpu.VMEM), pl.BlockSpec(memory_space=pltpu.SMEM)
    params = pltpu.CompilerParams(vmem_limit_bytes=VMEM_LIMIT)

    mine = lax.dynamic_slice_in_dim(obs_owner, my_index * leaf_dev, leaf_dev)
    leaf_at = jnp.arange(leaf_dev, dtype=jnp.int32)
    same = (mine[:, None] == mine[None, :]) & (leaf_at[None, :] < leaf_at[:, None])
    rank = jnp.sum(same.astype(jnp.int32), axis=1)
    rim_rows = from_behind(parent_local[parent_local.shape[0] - RIM :], AXES, 1)
    packed = pl.pallas_call(
        functools.partial(pack_sources, capacity),
        out_shape=jax.ShapeDtypeStruct((n_dev * block_rows, points), F32),
        in_specs=[smem, smem, smem, vmem, vmem],
        out_specs=vmem,
        compiler_params=params,
        name="pack_sources",
    )(mine, rank, leaf_center.T.reshape(-1), src_coords.transpose(1, 0, 2), src_charge)
    packed, rim_rows, obs_owner, near_slots = lax.optimization_barrier(
        (packed, rim_rows, obs_owner, near_slots)
    )
    counts = jnp.sum((obs_owner.reshape(n_dev, leaf_dev) == my_index).astype(jnp.int32), axis=1)
    live = (jnp.arange(capacity, dtype=jnp.int32)[None, :] < counts[:, None]).astype(jnp.int32).reshape(slot_table)

    live = live.reshape(slot_table // points, points)
    slots = near_slots.reshape(-1)
    recv = lax.all_to_all(
        packed.reshape(n_dev, block_rows, points), AXES, split_axis=0, concat_axis=0, tiled=True
    ).reshape(n_dev * block_rows, points)

    parents = jnp.concatenate([rim_rows, parent_local], axis=0)
    moved = jnp.einsum("pr,oqr->opq", parents, l2l_ops, precision=lax.Precision.HIGHEST)
    stacked = moved.reshape(8 * parents.shape[0], width)
    leaf_local, packed_dens = pl.pallas_call(
        route_leaves,
        out_shape=(
            jax.ShapeDtypeStruct((leaf_dev, width), F32),
            jax.ShapeDtypeStruct((slot_table, lanes), F32),
        ),
        in_specs=[smem, smem, vmem, vmem],
        out_specs=(vmem, vmem),
        compiler_params=params,
        name="route_leaves",
    )(child_octant * parents.shape[0] + parent_slot, mine * capacity + rank, child_m2l, stacked)
    packed_dens, slots, live = lax.optimization_barrier((packed_dens, slots, live))
    dens = lax.all_to_all(
        packed_dens.reshape(n_dev, capacity, lanes), AXES, split_axis=0, concat_axis=0, tiled=True
    ).reshape(slot_table, lanes)

    obs = obs_offset.transpose(1, 0, 2)
    pairs = slot_table * near_slots.shape[1] * points * points
    near = pl.pallas_call(
        functools.partial(near_kernel, capacity),
        out_shape=jax.ShapeDtypeStruct((slot_table, points), F32),
        in_specs=[smem, vmem, vmem, vmem, vmem],
        out_specs=vmem,
        scratch_shapes=[
            pltpu.VMEM((slot_table, FEATS, points), BF16),
            pltpu.VMEM((slot_table, FEATS, points), BF16),
            pltpu.VMEM((slot_table, points), F32),
            pltpu.VMEM((GROUP, points, FEATS), BF16),
            pltpu.VMEM((GROUP, points, FEATS), BF16),
            pltpu.VMEM((GROUP, points, points), F32),
            pltpu.VMEM((GROUP, points, points), F32),
        ],
        compiler_params=params,
        cost_estimate=pl.CostEstimate(flops=70 * pairs, bytes_accessed=5 * 10**6, transcendentals=pairs),
        name="near_field",
    )(
        slots,
        recv,
        obs,
        jnp.asarray(spread_matrix(SOURCE_ORDER, False)),
        jnp.asarray(spread_matrix(TARGET_ORDER, True)),
    )
    potential = pl.pallas_call(
        far_kernel,
        out_shape=jax.ShapeDtypeStruct((slot_table, points), F32),
        in_specs=[vmem, vmem, vmem, vmem],
        out_specs=vmem,
        scratch_shapes=[
            pltpu.VMEM((lanes, points), F32),
            pltpu.VMEM((3, points, points), F32),
            pltpu.VMEM((points, points), F32),
        ],
        compiler_params=params,
        cost_estimate=pl.CostEstimate(flops=10**10, bytes_accessed=5 * 10**6, transcendentals=10**7),
        name="far_field",
    )(dens, obs, near, live)
    return (leaf_local, potential)


def solution(mesh):
    placed = (
        P(AXES, None),
        P(AXES),
        P(AXES),
        P(AXES, None),
        P(),
        P(AXES, None),
        P(AXES, None, None),
        P(AXES, None),
        P(),
        P(AXES, None, None),
        P(AXES, None),
    )
    return jax.shard_map(
        on_device,
        mesh=mesh,
        in_specs=placed,
        out_specs=(P(AXES, None), P(AXES, None)),
        check_vma=False,
    )
```
